256 devices in a mesh: agent: 32 (over y, x, core), env: 8 (over z).
Axes of the slice: x: 4, y: 4, z: 8, core: 2. Of those that a mesh axis runs over, the one named last changes fastest.
Arguments:
- obs_rep: bfloat16 [8, 8192, 1024], P('env', 'agent'), may hold values from -6 to 6
- actions: int32 [8, 8192], P('env', 'agent'), may hold values from 0 to 31
- action_table: bfloat16 [32, 1024], replicated, may hold values from -6 to 6
- decode_rank: int32 [64], replicated, may hold values from 0 to 63, each once
- visible: int32 [64, 64], replicated, may hold values 0 or 1
- w_query: bfloat16 [1024, 1024], replicated, may hold values from -1 to 1
- w_key: bfloat16 [1024, 1024], replicated, may hold values from -1 to 1
- w_value: bfloat16 [1024, 1024], replicated, may hold values from -0.1875 to 0.1875
- w_out: bfloat16 [1024, 1024], replicated, may hold values from -0.1875 to 0.1875
- norm_gain: float32 [1024], replicated, may hold values from 0.5 to 1.5
- w_mix: bfloat16 [1024, 512], replicated, may hold values from -0.1875 to 0.1875
- w_group: bfloat16 [1024, 512], replicated, may hold values from -0.1875 to 0.1875
- w_head: float32 [512], replicated, may hold values from -0.25 to 0.25
- returns: float32 [8, 8192], P(None, ('agent', 'env')), may hold values from -6 to 6
- group_of_env: int32 [8], replicated, may hold values from 0 to 3, as said below
Outputs:
- value: float32 [8, 8192], P(None, ('agent', 'env'))
- advantage: float32 [8, 8192], P(None, ('agent', 'env'))
The draws below stay inside these ranges and needn't reach their ends.
Inputs may be any that keep to these rules, and one draw needn't show every extreme that they name: `group_of_env`: each group number names exactly 2 environments. `decode_rank`: each block's position occurs once.
All inputs are finite; a program needn't handle non-finite values.
Results may differ from the reference program's by a relative error of at most 0.01.
Values may be sent and summed in bfloat16 or wider, within the bound.
A program may use at most 384 MiB of HBM per device.

```python
import math
import jax
import jax.numpy as jnp
from jax import lax

D = 1024
H = 16
VH = 512
ACTS = 32
BLK = 128
GROUP = 2
NB = 64
AGENTS = 8192
ENVS = 8


def shared_weights(key):
    spread = D ** (-0.5)
    first = jnp.clip(jax.random.normal(jax.random.fold_in(key, 101), (D, D), jnp.float32), -6.0, 6.0) * spread
    second = jnp.clip(jax.random.normal(jax.random.fold_in(key, 102), (D, D), jnp.float32), -6.0, 6.0) * spread
    column = jax.random.randint(jax.random.fold_in(key, 103), (), 0, D)
    return (first, second, column)


def draw_w_query(key, part):
    first, second, column = shared_weights(key)
    return first.astype(jnp.bfloat16)


def draw_w_key(key, part):
    first, second, column = shared_weights(key)
    return second.astype(jnp.bfloat16)


def draw_obs_rep(key, part):
    first, second, column = shared_weights(key)
    key = jax.random.fold_in(key, 5)
    drawn = jnp.clip(jax.random.normal(jax.random.fold_in(key, 1), (ENVS, AGENTS, D), jnp.float32), -6.0, 6.0)
    query_dir = jnp.sign(lax.dynamic_index_in_dim(first, column, axis=1, keepdims=False))
    key_dir = jnp.sign(lax.dynamic_index_in_dim(second, column, axis=1, keepdims=False))
    unit = 2.0 / math.pi * D / math.sqrt(D // H)
    targets = jax.random.uniform(jax.random.fold_in(key, 2), (ENVS, AGENTS // BLK), jnp.float32, 130.0, 380.0)
    strength = jnp.sqrt(targets / unit)
    agent_ids = jnp.arange(AGENTS, dtype=jnp.int32)
    local = agent_ids % BLK
    block_ids = agent_ids // BLK
    level = jnp.take(strength, block_ids, axis=1)
    target_row = jnp.take(targets, block_ids, axis=1)
    key_factor = jnp.where(local[None, :] == 1, 1.0, jnp.where(local[None, :] == 2, 1.0 - 2.0 / target_row, 1.0 - 4.0 / target_row))
    is_key = (local >= 1) & (local <= 3)
    query_factor = jnp.where(local == BLK // 2, 1.0, 0.6)
    is_query = (local == BLK // 2) | (local == BLK // 2 + 1)
    key_rows = (level * key_factor)[:, :, None] * key_dir[None, None, :]
    query_rows = (level * query_factor[None, :])[:, :, None] * query_dir[None, None, :]
    result = jnp.where(is_key[None, :, None], key_rows, jnp.where(is_query[None, :, None], query_rows, drawn))
    return result.astype(jnp.bfloat16)


def draw_group_of_env(key, part):
    key = jax.random.fold_in(key, 7)
    order = jax.random.permutation(key, ENVS)
    return (order // GROUP).astype(jnp.int32)


def plant(entries, stream_key, low, top_value):
    place = [jax.random.randint(jax.random.fold_in(stream_key, axis), (), 0, length) for axis, length in enumerate(entries.shape)]
    widest = entries.shape.index(max(entries.shape))
    beside = place[:widest] + [(place[widest] + 1) % entries.shape[widest]] + place[widest + 1:]
    return entries.at[tuple(place)].set(low).at[tuple(beside)].set(top_value)


def shard_levels(stream_key, dims, shards, least, top_value):
    def one(dim, blocks):
        heights = jax.random.uniform(jax.random.fold_in(jax.random.fold_in(stream_key, 6), dim), (blocks,), jnp.float32, least / len(shards), top_value / len(shards))
        return jnp.repeat(jnp.exp(heights), dims[dim] // blocks).reshape((-1,) + (1,) * (len(dims) - dim - 1))

    factor_of = one(*shards[0])
    for cut in shards[1:]:
        factor_of = factor_of * one(*cut)
    return factor_of


def normal_values(own_key, dims, scale, limit, split=(), held_as=jnp.bfloat16):
    values = jax.random.normal(own_key, dims, jnp.float32) * scale
    if len(split) > 0:
        values = shard_levels(own_key, dims, split, -0.22, 0.18) * values
    return jnp.clip(values, min=-limit, max=limit).astype(held_as)


def setup_inputs(seed: int = 0) -> dict:
    key_list = jax.random.split(jax.random.key(seed), 16)
    obs_rep = draw_obs_rep(jax.random.fold_in(key_list[15], 71), 0)
    actions = plant(jax.random.randint(key_list[1], (ENVS, AGENTS), 0, ACTS), jax.random.fold_in(key_list[1], 1), 0, ACTS - 1).astype(jnp.int32)
    action_table = normal_values(key_list[2], (ACTS, D), 1.0, 6.0)
    decode_rank = jax.random.permutation(key_list[3], NB).astype(jnp.int32)
    visible = plant((jax.random.randint(key_list[4], (NB, NB), 0, 4) < 3).astype(jnp.int32), jax.random.fold_in(key_list[4], 1), 0, 1)
    w_query = draw_w_query(jax.random.fold_in(key_list[15], 71), 0)
    w_key = draw_w_key(jax.random.fold_in(key_list[15], 71), 0)
    w_value = normal_values(key_list[7], (D, D), D ** -0.5, 0.1875)
    w_out = normal_values(key_list[8], (D, D), D ** -0.5, 0.1875)
    norm_gain = jnp.clip(1.0 + 0.1 * jax.random.normal(key_list[9], (D,), jnp.float32), 0.5, 1.5)
    w_mix = normal_values(key_list[10], (D, VH), D ** -0.5, 0.1875)
    w_group = normal_values(key_list[11], (D, VH), D ** -0.5, 0.1875)
    w_head = normal_values(key_list[12], (VH,), VH ** -0.5, 0.25, (), jnp.float32)
    returns = normal_values(key_list[13], (ENVS, AGENTS), 1.0, 6.0, ((1, 256),), jnp.float32)
    group_of_env = draw_group_of_env(jax.random.fold_in(key_list[15], 71), 0)
    return {"obs_rep": obs_rep, "actions": actions, "action_table": action_table, "decode_rank": decode_rank, "visible": visible, "w_query": w_query, "w_key": w_key, "w_value": w_value, "w_out": w_out, "norm_gain": norm_gain, "w_mix": w_mix, "w_group": w_group, "w_head": w_head, "returns": returns, "group_of_env": group_of_env}


def visibility_mask(decode_rank, visible):
    agent_ids = jnp.arange(AGENTS, dtype=jnp.int32)
    block_ids = agent_ids // BLK
    ranking = decode_rank[block_ids]
    same_block = block_ids[:, None] == block_ids[None, :]
    causal = agent_ids[:, None] >= agent_ids[None, :]
    earlier = ranking[None, :] < ranking[:, None]
    allowed = visible[block_ids[:, None], block_ids[None, :]] == 1
    return same_block & causal | earlier & allowed

def decode_env(observed, tokens, mask, w_query, w_key, w_value, w_out, norm_gain):
    head_dim = D // H
    queries = jnp.dot(observed, w_query, preferred_element_type=jnp.float32).astype(jnp.bfloat16)
    keys_all = jnp.dot(tokens, w_key, preferred_element_type=jnp.float32).astype(jnp.bfloat16)
    values_all = jnp.dot(tokens, w_value, preferred_element_type=jnp.float32).astype(jnp.bfloat16)
    queries = queries.reshape(AGENTS, H, head_dim).astype(jnp.float32)
    keys_all = keys_all.reshape(AGENTS, H, head_dim).astype(jnp.float32)
    values_all = values_all.reshape(AGENTS, H, head_dim).astype(jnp.float32)
    scores = jnp.einsum('ahd,bhd->hab', queries, keys_all) * head_dim ** (-0.5)
    masked = jnp.where(mask[None], scores, -1e+30)
    peak = lax.optimization_barrier(jnp.max(masked, axis=2, keepdims=True))
    expo = jnp.where(mask[None], jnp.exp(masked - peak), 0.0)
    total = lax.optimization_barrier(jnp.sum(expo, axis=2))
    weights = expo.astype(jnp.bfloat16).astype(jnp.float32)
    mixed = jnp.einsum('hab,bhd->ahd', weights, values_all)
    attended = (mixed / jnp.transpose(total)[:, :, None]).astype(jnp.bfloat16).reshape(AGENTS, D)
    resid = observed.astype(jnp.float32) + jnp.dot(attended, w_out, preferred_element_type=jnp.float32)
    factor = lax.rsqrt(lax.optimization_barrier(jnp.mean(resid * resid, axis=1, keepdims=True)) + 1e-05)
    return (resid * factor * norm_gain).astype(jnp.bfloat16)

def reference(obs_rep, actions, action_table, decode_rank, visible, w_query, w_key, w_value, w_out, norm_gain, w_mix, w_group, w_head, returns, group_of_env):
    embedded = action_table[actions].astype(jnp.float32)
    tokens = (obs_rep.astype(jnp.float32) + embedded).astype(jnp.bfloat16)
    mask = visibility_mask(decode_rank, visible)

    def one_env(pair):
        return decode_env(pair[0], pair[1], mask, w_query, w_key, w_value, w_out, norm_gain)
    hidden = lax.map(one_env, (obs_rep, tokens))
    hidden_wide = hidden.astype(jnp.float32)
    mix = jnp.einsum('ead,dv->eav', hidden_wide, w_mix.astype(jnp.float32))
    part = jnp.einsum('ead,dv->eav', hidden_wide, w_group.astype(jnp.float32))
    same = (group_of_env[:, None] == group_of_env[None, :]).astype(jnp.float32) / GROUP
    centred = jnp.einsum('ef,fav->eav', same, part, precision=lax.Precision.HIGHEST)
    activ = jax.nn.gelu(mix + centred, approximate=False)
    value = jnp.einsum('eav,v->ea', activ, w_head, precision=lax.Precision.HIGHEST)
    excess = returns - value
    advantage = excess - jnp.dot(same, excess, precision=lax.Precision.HIGHEST)
    return (value, advantage)
```

```python
import functools

import jax
import jax.numpy as jnp
import numpy as np
from jax import lax
from jax.experimental import pallas as pl
from jax.experimental.pallas import tpu as pltpu
from jax.sharding import PartitionSpec as P

H = 16
BLK = 128
HALF = BLK // 2
HD = 64
LOG2E = 1.4426950408889634
NEG = -1e30
VROWS = 80
QN = 256
SIDE = 4
MESH = pl.DeviceIdType.MESH
BF = jnp.bfloat16
F32 = jnp.float32


def agent_at(y, x, core):
    return (y * SIDE + x) * 2 + core


def greet_plane(me):
    barrier = pltpu.get_barrier_semaphore()

    def tell(step, _):
        other = lax.rem(me + step, 2 * SIDE * SIDE)
        pl.semaphore_signal(barrier, inc=1, device_id={"agent": other}, device_id_type=MESH)
        return 0

    lax.fori_loop(1, 2 * SIDE * SIDE, tell, 0)
    return barrier


def project_kernel(
    obs_ref, act_ref, table_ref, wq_hbm, wk_hbm, wv_hbm,
    qbuf, kbuf, vbuf,
    wq, wk, wv, tok, kst, vst, qst, load_sem,
    ks_send, ks_recv, vs_send, vs_recv, qs_send, qs_recv, kf_send, kf_recv, vf_send, vf_recv, local_sem,
):
    me = lax.axis_index("agent")
    core = lax.rem(me, 2)
    chip = me // 2
    my_y, my_x = chip // SIDE, lax.rem(chip, SIDE)
    chips = SIDE * SIDE
    sibling = chip * 2 + 1 - core
    loads = [
        pltpu.make_async_copy(src, dst, load_sem.at[n])
        for n, (src, dst) in enumerate(((wk_hbm, wk), (wv_hbm, wv), (wq_hbm, wq)))
    ]
    for load in loads:
        load.start()
    barrier = greet_plane(me)

    onehot = (act_ref[...] == lax.broadcasted_iota(jnp.int32, (table_ref.shape[0], 2 * BLK), 0)).astype(F32)
    onehot = jnp.transpose(onehot).astype(BF)
    width = obs_ref.shape[1]
    part = 256

    def embed(n, _):
        cols = pl.ds(pl.multiple_of(n * part, part), part)
        added = jnp.dot(onehot, table_ref[:, cols], preferred_element_type=F32)
        tok[:, cols] = (obs_ref[:, cols].astype(F32) + added).astype(BF)
        return 0

    lax.fori_loop(0, width // part, embed, 0)

    def project(rows, w, out):
        def one(n, _):
            cols = pl.ds(pl.multiple_of(n * part, part), part)
            got = jnp.dot(rows, w[:, cols], preferred_element_type=F32).astype(BF)
            turned = jnp.transpose(got)
            out[0, cols, :] = turned[:, :BLK]
            out[1, cols, :] = turned[:, BLK:]
            return 0

        lax.fori_loop(0, width // part, one, 0)

    def there(step):
        return lax.rem(my_y + step // SIDE, SIDE), lax.rem(my_x + lax.rem(step, SIDE), SIDE)

    def back(step):
        return lax.rem(my_y + SIDE - step // SIDE, SIDE), lax.rem(my_x + SIDE - lax.rem(step, SIDE), SIDE)

    def head_rows(y, x):
        return pl.ds(pl.multiple_of((y * SIDE + x) * HD, HD), HD)

    def send(stage, buf, sends, recvs, step):
        y, x = there(step)
        return pltpu.make_async_remote_copy(
            src_ref=stage.at[:, head_rows(y, x), :],
            dst_ref=buf.at[pl.ds(me * 2, 2)],
            send_sem=sends.at[step], recv_sem=recvs.at[step],
            device_id={"agent": agent_at(y, x, core)}, device_id_type=MESH,
        )

    def arrival(stage, buf, sends, recvs, step):
        y, x = back(step)
        return pltpu.make_async_remote_copy(
            src_ref=stage.at[:, head_rows(y, x), :],
            dst_ref=buf.at[pl.ds(agent_at(y, x, core) * 2, 2)],
            send_sem=sends.at[step], recv_sem=recvs.at[step],
            device_id={"agent": agent_at(y, x, core)}, device_id_type=MESH,
        )

    def own_forward(stage, buf, sends, recvs):
        return pltpu.make_async_remote_copy(
            src_ref=stage.at[:, head_rows(my_y, my_x), :],
            dst_ref=buf.at[pl.ds(me * 2, 2)],
            send_sem=sends.at[0], recv_sem=recvs.at[0],
            device_id={"agent": sibling}, device_id_type=MESH,
        )

    def forward(buf, sends, recvs, step):
        y, x = back(step)
        slot = pl.ds(agent_at(y, x, core) * 2, 2)
        return pltpu.make_async_remote_copy(
            src_ref=buf.at[slot], dst_ref=buf.at[slot],
            send_sem=sends.at[step], recv_sem=recvs.at[step],
            device_id={"agent": sibling}, device_id_type=MESH,
        )

    def forwarded(buf, sends, recvs, step):
        y, x = back(step)
        slot = pl.ds(agent_at(y, x, 1 - core) * 2, 2)
        return pltpu.make_async_remote_copy(
            src_ref=buf.at[slot], dst_ref=buf.at[slot],
            send_sem=sends.at[step], recv_sem=recvs.at[step],
            device_id={"agent": sibling}, device_id_type=MESH,
        )

    def local(stage, buf, n):
        return pltpu.make_async_copy(
            stage.at[:, head_rows(my_y, my_x), :], buf.at[pl.ds(me * 2, 2)], local_sem.at[n]
        )

    def send_all(stage, buf, sends, recvs, fsends, frecvs, n):
        local(stage, buf, n).start()
        own_forward(stage, buf, fsends, frecvs).start()

        def one(step, _):
            send(stage, buf, sends, recvs, step).start()
            return 0

        lax.fori_loop(1, chips, one, 0)

    def q_send(step, flip):
        y, x = there(step)
        target = lax.rem(core + flip, 2)
        return pltpu.make_async_remote_copy(
            src_ref=qst.at[target, head_rows(y, x), :],
            dst_ref=qbuf.at[me],
            send_sem=qs_send.at[flip * chips + step], recv_sem=qs_recv.at[flip * chips + step],
            device_id={"agent": agent_at(y, x, target)}, device_id_type=MESH,
        )

    def q_arrival(step, flip):
        y, x = back(step)
        source = agent_at(y, x, lax.rem(core + flip, 2))
        return pltpu.make_async_remote_copy(
            src_ref=qst.at[core, head_rows(y, x), :],
            dst_ref=qbuf.at[source],
            send_sem=qs_send.at[flip * chips + step], recv_sem=qs_recv.at[flip * chips + step],
            device_id={"agent": source}, device_id_type=MESH,
        )

    loads[0].wait()
    project(tok[...], wk, kst)
    pl.semaphore_wait(barrier, 2 * chips - 1)
    send_all(kst, kbuf, ks_send, ks_recv, kf_send, kf_recv, 0)
    loads[1].wait()
    project(tok[...], wv, vst)
    send_all(vst, vbuf, vs_send, vs_recv, vf_send, vf_recv, 1)
    rows = jnp.concatenate(
        [obs_ref[0:HALF], obs_ref[BLK : BLK + HALF], obs_ref[HALF:BLK], obs_ref[BLK + HALF :]], axis=0
    )
    loads[2].wait()
    project(rows, wq, qst)
    q_local = pltpu.make_async_copy(qst.at[core, head_rows(my_y, my_x), :], qbuf.at[me], local_sem.at[2])
    q_local.start()
    q_send(0, 1).start()

    def q_one(step, _):
        q_send(step, 0).start()
        q_send(step, 1).start()
        return 0

    lax.fori_loop(1, chips, q_one, 0)

    def pass_on(stage, buf, sends, recvs, fsends, frecvs):
        def one(step, _):
            arrival(stage, buf, sends, recvs, step).wait_recv()
            forward(buf, fsends, frecvs, step).start()
            return 0

        lax.fori_loop(1, chips, one, 0)

    pass_on(kst, kbuf, ks_send, ks_recv, kf_send, kf_recv)
    pass_on(vst, vbuf, vs_send, vs_recv, vf_send, vf_recv)

    local(kst, kbuf, 0).wait()
    local(vst, vbuf, 1).wait()
    q_local.wait()
    own_forward(kst, kbuf, kf_send, kf_recv).wait_send()
    own_forward(vst, vbuf, vf_send, vf_recv).wait_send()
    forwarded(kbuf, kf_send, kf_recv, 0).wait_recv()
    forwarded(vbuf, vf_send, vf_recv, 0).wait_recv()
    q_send(0, 1).wait_send()
    q_arrival(0, 1).wait_recv()

    def finish(step, _):
        send(kst, kbuf, ks_send, ks_recv, step).wait_send()
        send(vst, vbuf, vs_send, vs_recv, step).wait_send()
        forward(kbuf, kf_send, kf_recv, step).wait_send()
        forward(vbuf, vf_send, vf_recv, step).wait_send()
        forwarded(kbuf, kf_send, kf_recv, step).wait_recv()
        forwarded(vbuf, vf_send, vf_recv, step).wait_recv()
        for flip in range(2):
            q_send(step, flip).wait_send()
            q_arrival(step, flip).wait_recv()
        return 0

    lax.fori_loop(1, chips, finish, 0)


def project(obs, actions, table, w_query, w_key, w_value):
    rows, width = obs.shape
    devices = 2 * SIDE * SIDE
    chips = SIDE * SIDE
    vm = pl.BlockSpec(memory_space=pltpu.VMEM)
    hbm = pl.BlockSpec(memory_space=pl.ANY)
    dma = pltpu.SemaphoreType.DMA
    return pl.pallas_call(
        project_kernel,
        out_shape=(
            jax.ShapeDtypeStruct((devices, HD, BLK), BF),
            jax.ShapeDtypeStruct((2 * devices, HD, BLK), BF),
            jax.ShapeDtypeStruct((2 * devices, HD, BLK), BF),
        ),
        in_specs=[vm, vm, vm] + [pl.BlockSpec(memory_space=pltpu.HBM)] * 3,
        out_specs=(hbm, hbm, hbm),
        scratch_shapes=[pltpu.VMEM((width, width), BF)] * 3
        + [pltpu.VMEM((rows, width), BF)]
        + [pltpu.VMEM((2, width, BLK), BF)] * 3
        + [dma((3,))]
        + [dma((chips,))] * 4
        + [dma((2 * chips,))] * 2
        + [dma((chips,))] * 4
        + [dma((3,))],
        compiler_params=pltpu.CompilerParams(
            collective_id=0, has_side_effects=True, vmem_limit_bytes=60 * 2**20
        ),
        name="project_and_send",
    )(obs, actions, table, w_query, w_key, w_value)


def attention_kernel(
    groups, steps,
    rank_ref, tile_ref, chunk_ref, rank_row, visible_ref, q_ref, k_ref, v_ref,
    o_ref,
    order, ks, vs, qa, acc, osort, sa, sb, mask,
):
    core = lax.rem(lax.axis_index("agent"), 2)
    blocks = k_ref.shape[0]
    per_tile = 4 * groups
    chunk_blocks = per_tile
    keys = chunk_blocks * BLK

    def place(b, _):
        order[rank_ref[b]] = b
        return 0

    lax.fori_loop(0, blocks, place, 0, unroll=4)

    lane = lax.broadcasted_iota(jnp.int32, (BLK, HD), 1)
    row = lax.broadcasted_iota(jnp.int32, (VROWS - HD, BLK), 0)
    ones = jnp.where(row == 0, 1.0, 0.0).astype(BF)

    def prepare(r, _):
        b = order[r]
        at = pl.multiple_of(r * BLK, BLK)
        hot = jnp.where(lane == r, 1.0, 0.0).astype(BF)
        ks[pl.ds(at, BLK), :] = jnp.concatenate([jnp.transpose(k_ref[b]), hot], axis=1)
        vs[r] = jnp.concatenate([v_ref[b], ones], axis=0)
        return 0

    lax.fori_loop(0, blocks, prepare, 0, unroll=4)

    ids_r = lax.broadcasted_iota(jnp.int32, (blocks, blocks), 0)
    ids_c = lax.broadcasted_iota(jnp.int32, (blocks, blocks), 1)
    to_rank = (ids_r == rank_row[...]).astype(BF)
    vis = visible_ref[...].astype(F32).astype(BF)
    by_query = jnp.dot(to_rank, vis, preferred_element_type=F32).astype(BF)
    ranked = lax.dot_general(
        by_query, to_rank, (((1,), (1,)), ((), ())), preferred_element_type=F32
    )
    sees = ((ids_r > ids_c) & (ranked > 0.5)) | (ids_r == ids_c)
    sees = jnp.transpose(jnp.where(sees, 1.0, 0.0)).astype(BF)

    qlane = lax.broadcasted_iota(jnp.int32, (HD, BLK), 1)
    spread_r = lax.broadcasted_iota(jnp.int32, (blocks, QN), 0)
    spread_c = lax.broadcasted_iota(jnp.int32, (blocks, QN), 1)

    def half(r, want):
        b = order[r]
        x = q_ref[b // 2].astype(F32)
        return jnp.where(jnp.full(x.shape, lax.rem(b, 2), jnp.int32) == want, x, pltpu.roll(x, HALF, 1))

    def prepare_queries(t, _):
        pieces = []
        for p in range(2):
            pieces.append(jnp.where(qlane < HALF, half(4 * t + 2 * p, 0), half(4 * t + 2 * p + 1, 1)))
        turned = (jnp.concatenate(pieces, axis=1) * HD**-0.5).astype(BF)
        spread = (spread_r == 4 * t + spread_c // HALF).astype(BF)
        open_ = jnp.dot(sees, spread, preferred_element_type=F32)
        bias = jnp.where(open_ > 0.5, 0.0, NEG).astype(BF)
        qa[t] = jnp.concatenate([turned, bias], axis=0)
        return 0

    lax.fori_loop(0, blocks // 4, prepare_queries, 0, unroll=2)

    mrow = lax.broadcasted_iota(jnp.int32, (2 * BLK, BLK), 0)
    mcol = lax.broadcasted_iota(jnp.int32, (2 * BLK, BLK), 1)
    late = (mrow // BLK == mcol // HALF) & (lax.rem(mrow, BLK) > lax.rem(mcol, HALF) + core * HALF)
    mask[0] = jnp.zeros((2 * BLK, BLK), F32)
    mask[1] = jnp.where(late, NEG, 0.0)
    acc[...] = jnp.zeros_like(acc)

    def score(i, buf):
        t, c = tile_ref[i], chunk_ref[i]
        diagonal = jnp.where(t == c, 1, 0)
        base = pl.multiple_of(c * keys, keys)
        peaks = []
        for g in range(groups):
            full = jnp.dot(ks[pl.ds(base, keys), :], qa[t * groups + g], preferred_element_type=F32)
            peak = None
            for blk in range(0, chunk_blocks, 2):
                rows = full[blk * BLK : (blk + 2) * BLK]
                p = blk // 2 - 2 * g
                if 0 <= p < 2:
                    cols = [rows[:, :BLK], rows[:, BLK:]]
                    cols[p] = cols[p] + mask[diagonal]
                    rows = jnp.concatenate(cols, axis=1)
                buf[g, blk * BLK : (blk + 2) * BLK] = rows
                top = jnp.max(rows.reshape(2 * BLK // 8, 8, QN), axis=0)
                peak = top if peak is None else jnp.maximum(peak, top)
            peaks.append(jnp.max(peak, axis=0, keepdims=True))
        return tuple(peaks)

    def absorb(i, buf, peaks, running):
        t, c = tile_ref[i], chunk_ref[i]
        new = []
        for g in range(groups):
            old = jnp.where(jnp.full((1, QN), c, jnp.int32) == 0, NEG, running[g])
            top = jnp.maximum(old, peaks[g])
            shrink = jnp.exp2((old - top) * LOG2E)
            expo = jnp.exp2((buf[g] - top) * LOG2E).astype(BF)
            vals = jnp.concatenate([vs[c * chunk_blocks + j] for j in range(chunk_blocks)], axis=1)
            acc[g] = acc[g] * shrink + jnp.dot(vals, expo, preferred_element_type=F32)
            new.append(top)

        @pl.when(c == t)
        def _():
            for g in range(groups):
                a = acc[g]
                out = a[:HD] / a[HD : HD + 1]
                for j in range(4):
                    osort[t * per_tile + g * 4 + j] = out[:, j * HALF : (j + 1) * HALF]

        return tuple(new)

    def two(h, carry):
        peaks, running = carry
        later = score(2 * h + 1, sb)
        running = absorb(2 * h, sa, peaks, running)
        peaks = score(2 * h + 2, sa)
        running = absorb(2 * h + 1, sb, later, running)
        return peaks, running

    running = tuple(jnp.full((1, QN), NEG, F32) for _ in range(groups))
    lax.fori_loop(0, steps // 2, two, (score(0, sa), running))

    def unsort(a, _):
        pair = [osort[rank_ref[2 * a]], osort[rank_ref[2 * a + 1]]]
        o_ref[a] = jnp.concatenate(pair, axis=1).astype(BF)
        return 0

    lax.fori_loop(0, blocks // 2, unsort, 0, unroll=2)


def attention(rank, visible, q, k, v, groups=2):
    blocks = k.shape[0]
    tiles = blocks // (4 * groups)
    plan = [(t, c) for t in range(tiles) for c in range(t + 1)]
    steps = len(plan)
    assert steps % 2 == 0
    plan.append((0, 0))
    tile_of = jnp.asarray(np.array([t for t, _ in plan], np.int32))
    chunk_of = jnp.asarray(np.array([c for _, c in plan], np.int32))
    keys = 4 * groups * BLK
    sm = pl.BlockSpec(memory_space=pltpu.SMEM)
    vm = pl.BlockSpec(memory_space=pltpu.VMEM)
    return pl.pallas_call(
        functools.partial(attention_kernel, groups, steps),
        out_shape=jax.ShapeDtypeStruct((blocks // 2, HD, BLK), BF),
        in_specs=[sm] * 3 + [vm] * 5,
        out_specs=vm,
        scratch_shapes=[
            pltpu.SMEM((blocks,), jnp.int32),
            pltpu.VMEM((blocks * BLK, HD + blocks), BF),
            pltpu.VMEM((blocks, VROWS, BLK), BF),
            pltpu.VMEM((blocks // 4, HD + blocks, QN), BF),
            pltpu.VMEM((groups, VROWS, QN), F32),
            pltpu.VMEM((blocks, HD, HALF), F32),
            pltpu.VMEM((groups, keys, QN), F32),
            pltpu.VMEM((groups, keys, QN), F32),
            pltpu.VMEM((2, 2 * BLK, BLK), F32),
        ],
        compiler_params=pltpu.CompilerParams(vmem_limit_bytes=48 * 2**20),
        name="attention",
    )(rank, tile_of, chunk_of, rank[None, :], visible, q, k, v)


def head_kernel(
    group_ref, o_hbm, obs_ref, gain_ref, whead_ref, ret_ref, wo, wm, wg,
    val_ref, adv_ref,
    att, resid, hid, hbuf, mix, part,
    a_send, a_recv, z_send, z_recv, local_sem,
):
    me = lax.axis_index("agent")
    env = lax.axis_index("env")
    envs = hbuf.shape[0]
    core = lax.rem(me, 2)
    chip = me // 2
    my_y, my_x = chip // SIDE, lax.rem(chip, SIDE)
    chips = SIDE * SIDE
    barrier = greet_plane(me)

    def tell(step, _):
        other = lax.rem(env + step, envs)
        pl.semaphore_signal(barrier, inc=1, device_id={"env": other}, device_id_type=MESH)
        return 0

    lax.fori_loop(1, envs, tell, 0)
    pl.semaphore_wait(barrier, 2 * chips - 1 + envs - 1)

    def send(step, flip):
        y = lax.rem(my_y + step // SIDE, SIDE)
        x = lax.rem(my_x + lax.rem(step, SIDE), SIDE)
        target = agent_at(y, x, lax.rem(core + flip, 2))
        return pltpu.make_async_remote_copy(
            src_ref=o_hbm.at[target], dst_ref=att.at[core, chip],
            send_sem=a_send.at[flip * chips + step], recv_sem=a_recv.at[flip * chips + step],
            device_id={"agent": target}, device_id_type=MESH,
        )

    def arrival(step, flip):
        y = lax.rem(my_y + SIDE - step // SIDE, SIDE)
        x = lax.rem(my_x + SIDE - lax.rem(step, SIDE), SIDE)
        other = lax.rem(core + flip, 2)
        return pltpu.make_async_remote_copy(
            src_ref=o_hbm.at[me], dst_ref=att.at[other, y * SIDE + x],
            send_sem=a_send.at[flip * chips + step], recv_sem=a_recv.at[flip * chips + step],
            device_id={"agent": agent_at(y, x, other)}, device_id_type=MESH,
        )

    own = pltpu.make_async_copy(o_hbm.at[me], att.at[core, chip], local_sem.at[0])
    own.start()
    send(0, 1).start()

    def start(step, _):
        send(step, 0).start()
        send(step, 1).start()
        return 0

    lax.fori_loop(1, chips, start, 0)
    own.wait()
    arrival(0, 1).wait_recv()

    def land(step, _):
        arrival(step, 0).wait_recv()
        arrival(step, 1).wait_recv()
        return 0

    lax.fori_loop(1, chips, land, 0)

    width = obs_ref.shape[1]
    wide = 256
    for half in range(2):
        rows = jnp.transpose(att[half].reshape(width, BLK))
        seen = jnp.concatenate(
            [obs_ref[half * HALF : (half + 1) * HALF], obs_ref[BLK + half * HALF : BLK + (half + 1) * HALF]], axis=0
        ).astype(F32)
        for n in range(width // wide):
            cols = slice(n * wide, (n + 1) * wide)
            resid[half * BLK : (half + 1) * BLK, cols] = seen[:, cols] + jnp.dot(
                rows, wo[:, cols], preferred_element_type=F32
            )
    whole = resid[...]
    factor = lax.rsqrt(jnp.mean(whole * whole, axis=1, keepdims=True) + 1e-05)
    hid[...] = (whole * factor * gain_ref[...]).astype(BF)

    per_env = 2 * BLK // envs

    def piece(e):
        quarter = lax.rem(e, 4)
        return pl.ds(pl.multiple_of(quarter // 2 * BLK + e // 4 * HALF + lax.rem(quarter, 2) * per_env, per_env), per_env)

    def z_copy(step):
        other = lax.rem(env + step, envs)
        return pltpu.make_async_remote_copy(
            src_ref=hid.at[piece(other)], dst_ref=hbuf.at[env],
            send_sem=z_send.at[step], recv_sem=z_recv.at[step],
            device_id={"env": other}, device_id_type=MESH,
        )

    def z_arrival(step):
        other = lax.rem(env + envs - step, envs)
        return pltpu.make_async_remote_copy(
            src_ref=hid.at[piece(env)], dst_ref=hbuf.at[other],
            send_sem=z_send.at[step], recv_sem=z_recv.at[step],
            device_id={"env": other}, device_id_type=MESH,
        )

    mine = pltpu.make_async_copy(hid.at[piece(env)], hbuf.at[env], local_sem.at[1])
    mine.start()

    def z_start(step, _):
        z_copy(step).start()
        return 0

    lax.fori_loop(1, envs, z_start, 0)
    mine.wait()

    def z_land(step, _):
        z_arrival(step).wait_recv()
        return 0

    lax.fori_loop(1, envs, z_land, 0)

    moved = hbuf[...].reshape(envs * per_env, width)
    hidden_units = whead_ref.shape[1]
    for n in range(hidden_units // wide):
        cols = slice(n * wide, (n + 1) * wide)
        mix[:, :, cols] = jnp.dot(moved, wm[:, cols], preferred_element_type=F32).reshape(envs, per_env, wide)
        part[:, :, cols] = jnp.dot(moved, wg[:, cols], preferred_element_type=F32).reshape(envs, per_env, wide)
    partners = []
    values = []
    for e in range(envs):
        partner = jnp.int32(0)
        for f in range(envs):
            if f != e:
                partner = jnp.where(group_ref[f] == group_ref[e], f, partner)
        partners.append(partner)
        x = mix[e] + 0.5 * (part[e] + part[partner])
        activ = 0.5 * x * (1.0 + lax.erf(x * np.float32(np.sqrt(0.5))))
        values.append(jnp.sum(activ * whead_ref[...], axis=1, keepdims=True).T)
    for e in range(envs):
        val_ref[e : e + 1, :] = values[e]
    excess = ret_ref[...] - val_ref[...]
    rows = lax.broadcasted_iota(jnp.int32, (envs, per_env), 0)
    for e in range(envs):
        mine_ = excess[e : e + 1]
        other = jnp.sum(jnp.where(rows == jnp.full(rows.shape, partners[e], jnp.int32), excess, 0.0), axis=0, keepdims=True)
        adv_ref[e : e + 1, :] = mine_ - 0.5 * (mine_ + other)

    send(0, 1).wait_send()

    def finish(step, _):
        send(step, 0).wait_send()
        send(step, 1).wait_send()
        return 0

    lax.fori_loop(1, chips, finish, 0)

    def z_finish(step, _):
        z_copy(step).wait_send()
        return 0

    lax.fori_loop(1, envs, z_finish, 0)


def head(group_of_env, o, obs, gain, w_head, returns, w_out, w_mix, w_group):
    rows, width = obs.shape
    envs, per_env = returns.shape
    units = w_head.shape[0]
    chips = SIDE * SIDE
    sm = pl.BlockSpec(memory_space=pltpu.SMEM)
    vm = pl.BlockSpec(memory_space=pltpu.VMEM)
    hbm = pl.BlockSpec(memory_space=pl.ANY)
    dma = pltpu.SemaphoreType.DMA
    out = jax.ShapeDtypeStruct((envs, per_env), F32)
    return pl.pallas_call(
        head_kernel,
        out_shape=(out, out),
        in_specs=[sm, hbm] + [vm] * 7,
        out_specs=(vm, vm),
        scratch_shapes=[
            pltpu.VMEM((2, chips, HD, BLK), BF),
            pltpu.VMEM((rows, width), F32),
            pltpu.VMEM((rows, width), BF),
            pltpu.VMEM((envs, per_env, width), BF),
            pltpu.VMEM((envs, per_env, units), F32),
            pltpu.VMEM((envs, per_env, units), F32),
            dma((2 * chips,)),
            dma((2 * chips,)),
            dma((envs,)),
            dma((envs,)),
            dma((2,)),
        ],
        compiler_params=pltpu.CompilerParams(
            collective_id=1, has_side_effects=True, vmem_limit_bytes=40 * 2**20
        ),
        name="rows_and_value",
    )(group_of_env, o, obs, gain[None, :], w_head[None, :], returns, w_out, w_mix, w_group)


def on_device(
    obs_rep, actions, action_table, decode_rank, visible, w_query, w_key, w_value, w_out,
    norm_gain, w_mix, w_group, w_head, returns, group_of_env,
):
    obs = obs_rep[0]
    q, k, v = project(obs, actions, action_table, w_query, w_key, w_value)
    o = attention(decode_rank, visible, q, k, v)
    return head(group_of_env, o, obs, norm_gain, w_head, returns, w_out, w_mix, w_group)


def solution(mesh):
    spec = P(None, ("agent", "env"))
    in_specs = (P("env", "agent", None), P("env", "agent")) + (P(),) * 11 + (spec, P())
    return jax.shard_map(
        on_device, mesh=mesh, in_specs=in_specs, out_specs=(spec, spec), check_vma=False
    )
```

```python
import jax
import jax.numpy as jnp
import numpy as np
from jax import lax
from jax.experimental import pallas as pl
from jax.experimental.pallas import tpu as pltpu
from jax.sharding import PartitionSpec as P

H = 16
BLK = 128
HALF = BLK // 2
HD = 64
LOG2E = 1.4426950408889634
NEG = -1e30
VROWS = 80
QN = 256
SIDE = 4
MESH = pl.DeviceIdType.MESH
BF = jnp.bfloat16
F32 = jnp.float32


def agent_at(y, x, core):
    return (y * SIDE + x) * 2 + core


OFFSETS = (
    (0, 1), (0, 3), (1, 0), (3, 0), (0, 2), (2, 0), (1, 1), (3, 3),
    (1, 3), (3, 1), (1, 2), (3, 2), (2, 1), (2, 3), (2, 2),
)
RING = (1, 7, 2, 6, 3, 5, 4)


def pick(n, values):
    got = jnp.int32(values[0])
    for at, value in enumerate(values[1:], 1):
        got = jnp.where(n == at, value, got)
    return got


def chip_step(n):
    return pick(n, (0,) + tuple(y * SIDE + x for y, x in OFFSETS))


def decoder_kernel(
    rank_ref, order, group_ref, rank_row, visible_ref, obs_ref, act_ref, table_ref, gain_ref, whead_ref, ret_ref,
    wq_hbm, wk_hbm, wv_hbm, wo_hbm, wm_hbm, wg_hbm,
    val_ref, adv_ref,
    wq, wk, wv, wo, wm, wg, tok, kst, vst, qst, qbuf, kbuf, vbuf,
    ks, vs, qa, acc, osort, ost, sa, sb, mask,
    att, resid, hid, hbuf, mix, part,
    load_sem, ks_send, ks_recv, vs_send, vs_recv, qs_send, qs_recv, kf_send, kf_recv, vf_send, vf_recv,
    a_send, a_recv, z_send, z_recv, local_sem,
):
    groups = acc.shape[0]
    env = lax.axis_index("env")
    envs = hbuf.shape[0]
    me = lax.axis_index("agent")
    core = lax.rem(me, 2)
    chip = me // 2
    my_y, my_x = chip // SIDE, lax.rem(chip, SIDE)
    chips = SIDE * SIDE
    sibling = chip * 2 + 1 - core
    pairs = ((wk_hbm, wk), (wv_hbm, wv), (wq_hbm, wq), (wo_hbm, wo), (wm_hbm, wm), (wg_hbm, wg))
    loads = [pltpu.make_async_copy(src, dst, load_sem.at[n]) for n, (src, dst) in enumerate(pairs)]
    for load in loads[:3]:
        load.start()
    barrier = pltpu.get_barrier_semaphore()

    def tell(step, _):
        other = lax.rem(me + step, 2 * chips)
        pl.semaphore_signal(barrier, inc=1, device_id={"agent": other}, device_id_type=MESH)
        return 0

    def tell_env(step, _):
        other = lax.rem(env + step, envs)
        pl.semaphore_signal(barrier, inc=1, device_id={"env": other}, device_id_type=MESH)
        return 0

    lax.fori_loop(1, 2 * chips, tell, 0)
    lax.fori_loop(1, envs, tell_env, 0)

    blocks = rank_row.shape[1]
    ids_r = lax.broadcasted_iota(jnp.int32, (blocks, blocks), 0)
    ids_c = lax.broadcasted_iota(jnp.int32, (blocks, blocks), 1)
    to_rank = (ids_r == rank_row[...]).astype(F32)

    onehot = (act_ref[...] == lax.broadcasted_iota(jnp.int32, (table_ref.shape[0], 2 * BLK), 0)).astype(F32)
    onehot = jnp.transpose(onehot).astype(BF)
    width = obs_ref.shape[1]
    strip = 256

    def embed(n, _):
        cols = pl.ds(pl.multiple_of(n * strip, strip), strip)
        added = jnp.dot(onehot, table_ref[:, cols], preferred_element_type=F32)
        tok[:, cols] = (obs_ref[:, cols].astype(F32) + added).astype(BF)
        return 0

    lax.fori_loop(0, width // strip, embed, 0)

    def project(rows, w, out):
        def one(n, _):
            cols = pl.ds(pl.multiple_of(n * strip, strip), strip)
            got = jnp.dot(rows, w[:, cols], preferred_element_type=F32).astype(BF)
            turned = jnp.transpose(got)
            out[0, cols, :] = turned[:, :BLK]
            out[1, cols, :] = turned[:, BLK:]
            return 0

        lax.fori_loop(0, width // strip, one, 0)

    def there(step):
        return lax.rem(my_y + step // SIDE, SIDE), lax.rem(my_x + lax.rem(step, SIDE), SIDE)

    def back(step):
        return lax.rem(my_y + SIDE - step // SIDE, SIDE), lax.rem(my_x + SIDE - lax.rem(step, SIDE), SIDE)

    def head_rows(y, x):
        return pl.ds(pl.multiple_of((y * SIDE + x) * HD, HD), HD)

    def send(stage, buf, sends, recvs, step):
        y, x = there(step)
        return pltpu.make_async_remote_copy(
            src_ref=stage.at[:, head_rows(y, x), :],
            dst_ref=buf.at[pl.ds(me * 2, 2)],
            send_sem=sends.at[step], recv_sem=recvs.at[step],
            device_id={"agent": agent_at(y, x, core)}, device_id_type=MESH,
        )

    def arrival(stage, buf, sends, recvs, step):
        y, x = back(step)
        return pltpu.make_async_remote_copy(
            src_ref=stage.at[:, head_rows(y, x), :],
            dst_ref=buf.at[pl.ds(agent_at(y, x, core) * 2, 2)],
            send_sem=sends.at[step], recv_sem=recvs.at[step],
            device_id={"agent": agent_at(y, x, core)}, device_id_type=MESH,
        )

    def own_forward(stage, buf, sends, recvs):
        return pltpu.make_async_remote_copy(
            src_ref=stage.at[:, head_rows(my_y, my_x), :],
            dst_ref=buf.at[pl.ds(me * 2, 2)],
            send_sem=sends.at[0], recv_sem=recvs.at[0],
            device_id={"agent": sibling}, device_id_type=MESH,
        )

    def forward(buf, sends, recvs, step):
        y, x = back(step)
        slot = pl.ds(agent_at(y, x, core) * 2, 2)
        return pltpu.make_async_remote_copy(
            src_ref=buf.at[slot], dst_ref=buf.at[slot],
            send_sem=sends.at[step], recv_sem=recvs.at[step],
            device_id={"agent": sibling}, device_id_type=MESH,
        )

    def forwarded(buf, sends, recvs, step):
        y, x = back(step)
        slot = pl.ds(agent_at(y, x, 1 - core) * 2, 2)
        return pltpu.make_async_remote_copy(
            src_ref=buf.at[slot], dst_ref=buf.at[slot],
            send_sem=sends.at[step], recv_sem=recvs.at[step],
            device_id={"agent": sibling}, device_id_type=MESH,
        )

    def local(stage, buf, n):
        return pltpu.make_async_copy(
            stage.at[:, head_rows(my_y, my_x), :], buf.at[pl.ds(me * 2, 2)], local_sem.at[n]
        )

    def send_all(stage, buf, sends, recvs, fsends, frecvs, n):
        local(stage, buf, n).start()
        own_forward(stage, buf, fsends, frecvs).start()

        def one(n, _):
            send(stage, buf, sends, recvs, chip_step(n)).start()
            return 0

        lax.fori_loop(1, chips, one, 0)

    def q_send(step, flip):
        y, x = there(step)
        target = lax.rem(core + flip, 2)
        return pltpu.make_async_remote_copy(
            src_ref=qst.at[target, head_rows(y, x), :],
            dst_ref=qbuf.at[me],
            send_sem=qs_send.at[flip * chips + step], recv_sem=qs_recv.at[flip * chips + step],
            device_id={"agent": agent_at(y, x, target)}, device_id_type=MESH,
        )

    def q_arrival(step, flip):
        y, x = back(step)
        source = agent_at(y, x, lax.rem(core + flip, 2))
        return pltpu.make_async_remote_copy(
            src_ref=qst.at[core, head_rows(y, x), :],
            dst_ref=qbuf.at[source],
            send_sem=qs_send.at[flip * chips + step], recv_sem=qs_recv.at[flip * chips + step],
            device_id={"agent": source}, device_id_type=MESH,
        )

    loads[0].wait()
    project(tok[...], wk, kst)
    pl.semaphore_wait(barrier, 2 * chips - 1 + envs - 1)
    for load in loads[3:]:
        load.start()
    send_all(kst, kbuf, ks_send, ks_recv, kf_send, kf_recv, 0)
    loads[1].wait()
    project(tok[...], wv, vst)
    send_all(vst, vbuf, vs_send, vs_recv, vf_send, vf_recv, 1)
    rows = jnp.concatenate(
        [obs_ref[0:HALF], obs_ref[BLK : BLK + HALF], obs_ref[HALF:BLK], obs_ref[BLK + HALF :]], axis=0
    )
    loads[2].wait()
    project(rows, wq, qst)
    q_local = pltpu.make_async_copy(qst.at[core, head_rows(my_y, my_x), :], qbuf.at[me], local_sem.at[2])
    q_local.start()
    q_send(0, 1).start()

    def q_one(n, _):
        step = chip_step(n)
        q_send(step, 0).start()
        q_send(step, 1).start()
        return 0

    lax.fori_loop(1, chips, q_one, 0)

    def pass_on(stage, buf, sends, recvs, fsends, frecvs):
        def one(n, _):
            step = chip_step(n)
            arrival(stage, buf, sends, recvs, step).wait_recv()
            forward(buf, fsends, frecvs, step).start()
            return 0

        def two(step, _):
            forwarded(buf, fsends, frecvs, step).wait_recv()
            return 0

        lax.fori_loop(1, chips, one, 0)
        lax.fori_loop(0, chips, two, 0)

    lane = lax.broadcasted_iota(jnp.int32, (BLK, HD), 1)
    row = lax.broadcasted_iota(jnp.int32, (VROWS - HD, BLK), 0)
    ones = jnp.where(row == 0, 1.0, 0.0).astype(BF)

    def prepare_keys(r, _):
        at = pl.multiple_of(r * BLK, BLK)
        hot = jnp.where(lane == r, 1.0, 0.0).astype(BF)
        ks[pl.ds(at, BLK), :] = jnp.concatenate([jnp.transpose(kbuf[order[r]]), hot], axis=1)
        return 0

    def prepare_values(r, _):
        vs[r] = jnp.concatenate([vbuf[order[r]], ones], axis=0)
        return 0

    to_rank = to_rank.astype(BF)
    vis = visible_ref[...].astype(F32).astype(BF)
    by_query = jnp.dot(to_rank, vis, preferred_element_type=F32).astype(BF)
    ranked = lax.dot_general(
        by_query, to_rank, (((1,), (1,)), ((), ())), preferred_element_type=F32
    )
    sees = ((ids_r > ids_c) & (ranked > 0.5)) | (ids_r == ids_c)
    sees = jnp.transpose(jnp.where(sees, 1.0, 0.0)).astype(BF)

    mrow = lax.broadcasted_iota(jnp.int32, (2 * BLK, BLK), 0)
    mcol = lax.broadcasted_iota(jnp.int32, (2 * BLK, BLK), 1)
    late = (mrow // BLK == mcol // HALF) & (lax.rem(mrow, BLK) > lax.rem(mcol, HALF) + core * HALF)
    mask[0] = jnp.zeros((2 * BLK, BLK), F32)
    mask[1] = jnp.where(late, NEG, 0.0)
    acc[...] = jnp.zeros_like(acc)

    qlane = lax.broadcasted_iota(jnp.int32, (HD, BLK), 1)
    spread_r = lax.broadcasted_iota(jnp.int32, (blocks, QN), 0)
    spread_c = lax.broadcasted_iota(jnp.int32, (blocks, QN), 1)

    def half(r, want):
        b = order[r]
        x = qbuf[b // 2].astype(F32)
        return jnp.where(jnp.full(x.shape, lax.rem(b, 2), jnp.int32) == want, x, pltpu.roll(x, HALF, 1))

    def prepare_queries(t, _):
        pieces = []
        for p in range(2):
            pieces.append(jnp.where(qlane < HALF, half(4 * t + 2 * p, 0), half(4 * t + 2 * p + 1, 1)))
        turned = (jnp.concatenate(pieces, axis=1) * HD**-0.5).astype(BF)
        spread = (spread_r == 4 * t + spread_c // HALF).astype(BF)
        open_ = jnp.dot(sees, spread, preferred_element_type=F32)
        bias = jnp.where(open_ > 0.5, 0.0, NEG).astype(BF)
        qa[t] = jnp.concatenate([turned, bias], axis=0)
        return 0

    per_tile = 4 * groups
    chunk_blocks = per_tile
    keys = chunk_blocks * BLK
    tiles = blocks // per_tile

    def place_of(i):
        p, j = i // (tiles + 1), lax.rem(i, tiles + 1)
        first = j < p + 1
        return jnp.where(first, p, tiles - 1 - p), jnp.where(first, j, j - p - 1)

    pass_on(kst, kbuf, ks_send, ks_recv, kf_send, kf_recv)
    local(kst, kbuf, 0).wait()
    lax.fori_loop(0, blocks, prepare_keys, 0, unroll=4)
    pass_on(vst, vbuf, vs_send, vs_recv, vf_send, vf_recv)
    local(vst, vbuf, 1).wait()
    lax.fori_loop(0, blocks, prepare_values, 0, unroll=4)
    q_local.wait()
    q_arrival(0, 1).wait_recv()

    def q_land(step, _):
        q_arrival(step, 0).wait_recv()
        q_arrival(step, 1).wait_recv()
        return 0

    lax.fori_loop(1, chips, q_land, 0)
    lax.fori_loop(0, blocks // 4, prepare_queries, 0, unroll=2)

    def score(i, buf, which):
        t, c = place_of(i)
        diagonal = jnp.where(t == c, 1, 0)
        base = pl.multiple_of(c * keys, keys)
        peaks = []
        for g in which:
            full = jnp.dot(ks[pl.ds(base, keys), :], qa[t * groups + g], preferred_element_type=F32)
            peak = None
            for blk in range(0, chunk_blocks, 2):
                rows = full[blk * BLK : (blk + 2) * BLK]
                p = blk // 2 - 2 * g
                if 0 <= p < 2:
                    cols = [rows[:, :BLK], rows[:, BLK:]]
                    cols[p] = cols[p] + mask[diagonal]
                    rows = jnp.concatenate(cols, axis=1)
                buf[g, blk * BLK : (blk + 2) * BLK] = rows
                top = jnp.max(rows.reshape(2 * BLK // 8, 8, QN), axis=0)
                peak = top if peak is None else jnp.maximum(peak, top)
            peaks.append(jnp.max(peak, axis=0, keepdims=True))
        return tuple(peaks)

    def absorb(i, buf, peaks, running, which):
        t, c = place_of(i)
        new = []
        for g, peak, before in zip(which, peaks, running):
            old = jnp.where(jnp.full((1, QN), c, jnp.int32) == 0, NEG, before)
            top = jnp.maximum(old, peak)
            shrink = jnp.exp2((old - top) * LOG2E)
            expo = jnp.exp2((buf[g] - top) * LOG2E).astype(BF)
            vals = jnp.concatenate([vs[c * chunk_blocks + j] for j in range(chunk_blocks)], axis=1)
            acc[g] = acc[g] * shrink + jnp.dot(vals, expo, preferred_element_type=F32)
            new.append(top)

        return tuple(new)

    def finish_tile(i):
        t, c = place_of(i)

        @pl.when(c == t)
        def _():
            for g in range(groups):
                a = acc[g]
                out = a[:HD] / a[HD : HD + 1]
                for j in range(4):
                    osort[t * per_tile + g * 4 + j] = out[:, j * HALF : (j + 1) * HALF]

    def both(i, now, later, peaks, running):
        next_peaks, next_running = (), ()
        for g in range(groups):
            next_peaks += score(i + 1, later, (g,))
            next_running += absorb(i, now, peaks[g : g + 1], running[g : g + 1], (g,))
        finish_tile(i)
        return next_peaks, next_running

    def two(h, carry):
        peaks, running = both(2 * h, sa, sb, *carry)
        return both(2 * h + 1, sb, sa, peaks, running)

    running = tuple(jnp.full((1, QN), NEG, F32) for _ in range(groups))
    steps = tiles * (tiles + 1) // 2
    lax.fori_loop(0, steps // 2, two, (score(0, sa, range(groups)), running))

    def o_send(step, flip):
        y = lax.rem(my_y + step // SIDE, SIDE)
        x = lax.rem(my_x + lax.rem(step, SIDE), SIDE)
        target = agent_at(y, x, lax.rem(core + flip, 2))
        return pltpu.make_async_remote_copy(
            src_ref=ost.at[target], dst_ref=att.at[core, chip],
            send_sem=a_send.at[flip * chips + step], recv_sem=a_recv.at[flip * chips + step],
            device_id={"agent": target}, device_id_type=MESH,
        )

    def o_arrival(step, flip):
        y = lax.rem(my_y + SIDE - step // SIDE, SIDE)
        x = lax.rem(my_x + SIDE - lax.rem(step, SIDE), SIDE)
        other = lax.rem(core + flip, 2)
        return pltpu.make_async_remote_copy(
            src_ref=ost.at[me], dst_ref=att.at[other, y * SIDE + x],
            send_sem=a_send.at[flip * chips + step], recv_sem=a_recv.at[flip * chips + step],
            device_id={"agent": agent_at(y, x, other)}, device_id_type=MESH,
        )

    def unsort(target):
        pair = [osort[rank_ref[2 * target]], osort[rank_ref[2 * target + 1]]]
        ost[target] = jnp.concatenate(pair, axis=1).astype(BF)

    own = pltpu.make_async_copy(ost.at[me], att.at[core, chip], local_sem.at[3])
    unsort(sibling)
    o_send(0, 1).start()
    unsort(me)
    own.start()

    def start(n, _):
        step = chip_step(n)
        y, x = there(step)
        unsort(agent_at(y, x, 0))
        unsort(agent_at(y, x, 1))
        o_send(step, 0).start()
        o_send(step, 1).start()
        return 0

    lax.fori_loop(1, chips, start, 0)
    own.wait()
    o_arrival(0, 1).wait_recv()

    def land(step, _):
        o_arrival(step, 0).wait_recv()
        o_arrival(step, 1).wait_recv()
        return 0

    lax.fori_loop(1, chips, land, 0)

    loads[3].wait()
    wide = 256
    for half in range(2):
        rows = jnp.transpose(att[half].reshape(width, BLK))
        seen = jnp.concatenate(
            [obs_ref[half * HALF : (half + 1) * HALF], obs_ref[BLK + half * HALF : BLK + (half + 1) * HALF]], axis=0
        ).astype(F32)
        for n in range(width // wide):
            cols = slice(n * wide, (n + 1) * wide)
            resid[half * BLK : (half + 1) * BLK, cols] = seen[:, cols] + jnp.dot(
                rows, wo[:, cols], preferred_element_type=F32
            )
    whole = resid[...]
    factor = lax.rsqrt(jnp.mean(whole * whole, axis=1, keepdims=True) + 1e-05)
    hid[...] = (whole * factor * gain_ref[...]).astype(BF)

    per_env = 2 * BLK // envs

    def piece(e):
        quarter = lax.rem(e, 4)
        return pl.ds(pl.multiple_of(quarter // 2 * BLK + e // 4 * HALF + lax.rem(quarter, 2) * per_env, per_env), per_env)

    def z_copy(step):
        other = lax.rem(env + step, envs)
        return pltpu.make_async_remote_copy(
            src_ref=hid.at[piece(other)], dst_ref=hbuf.at[env],
            send_sem=z_send.at[step], recv_sem=z_recv.at[step],
            device_id={"env": other}, device_id_type=MESH,
        )

    def z_arrival(step):
        other = lax.rem(env + envs - step, envs)
        return pltpu.make_async_remote_copy(
            src_ref=hid.at[piece(env)], dst_ref=hbuf.at[other],
            send_sem=z_send.at[step], recv_sem=z_recv.at[step],
            device_id={"env": other}, device_id_type=MESH,
        )

    mine = pltpu.make_async_copy(hid.at[piece(env)], hbuf.at[env], local_sem.at[4])
    mine.start()

    def z_start(n, _):
        z_copy(pick(n, (0,) + RING)).start()
        return 0

    lax.fori_loop(1, envs, z_start, 0)
    mine.wait()

    def z_land(step, _):
        z_arrival(step).wait_recv()
        return 0

    lax.fori_loop(1, envs, z_land, 0)

    loads[4].wait()
    loads[5].wait()
    moved = hbuf[...].reshape(envs * per_env, width)
    hidden_units = whead_ref.shape[1]
    for n in range(hidden_units // wide):
        cols = slice(n * wide, (n + 1) * wide)
        mix[:, :, cols] = jnp.dot(moved, wm[:, cols], preferred_element_type=F32).reshape(envs, per_env, wide)
        part[:, :, cols] = jnp.dot(moved, wg[:, cols], preferred_element_type=F32).reshape(envs, per_env, wide)
    partners = []
    values = []
    for e in range(envs):
        partner = jnp.int32(0)
        for f in range(envs):
            if f != e:
                partner = jnp.where(group_ref[f] == group_ref[e], f, partner)
        partners.append(partner)
        x = mix[e] + 0.5 * (part[e] + part[partner])
        activ = 0.5 * x * (1.0 + lax.erf(x * np.float32(np.sqrt(0.5))))
        values.append(jnp.sum(activ * whead_ref[...], axis=1, keepdims=True).T)
    for e in range(envs):
        val_ref[e : e + 1, :] = values[e]
    excess = ret_ref[...] - val_ref[...]
    rows = lax.broadcasted_iota(jnp.int32, (envs, per_env), 0)
    for e in range(envs):
        mine_ = excess[e : e + 1]
        other = jnp.sum(jnp.where(rows == jnp.full(rows.shape, partners[e], jnp.int32), excess, 0.0), axis=0, keepdims=True)
        adv_ref[e : e + 1, :] = mine_ - 0.5 * (mine_ + other)

    own_forward(kst, kbuf, kf_send, kf_recv).wait_send()
    own_forward(vst, vbuf, vf_send, vf_recv).wait_send()
    q_send(0, 1).wait_send()
    o_send(0, 1).wait_send()

    def finish(step, _):
        send(kst, kbuf, ks_send, ks_recv, step).wait_send()
        send(vst, vbuf, vs_send, vs_recv, step).wait_send()
        forward(kbuf, kf_send, kf_recv, step).wait_send()
        forward(vbuf, vf_send, vf_recv, step).wait_send()
        for flip in range(2):
            q_send(step, flip).wait_send()
            o_send(step, flip).wait_send()
        return 0

    lax.fori_loop(1, chips, finish, 0)

    def z_finish(step, _):
        z_copy(step).wait_send()
        return 0

    lax.fori_loop(1, envs, z_finish, 0)


def decoder(rank, group_of_env, visible, obs, actions, table, gain, w_head, returns, w_query, w_key, w_value, w_out, w_mix, w_group):
    rows, width = obs.shape
    envs, per_env = returns.shape
    units = w_head.shape[0]
    blocks = rank.shape[0]
    chips = SIDE * SIDE
    groups = 2
    keys = 4 * groups * BLK
    ids = jnp.arange(blocks, dtype=jnp.int32)
    order = jnp.sum(jnp.where(rank[None, :] == ids[:, None], ids[None, :], 0), axis=1)
    sm = pl.BlockSpec(memory_space=pltpu.SMEM)
    vm = pl.BlockSpec(memory_space=pltpu.VMEM)
    hbm = pl.BlockSpec(memory_space=pl.ANY)
    dma = pltpu.SemaphoreType.DMA
    out = jax.ShapeDtypeStruct((envs, per_env), F32)
    return pl.pallas_call(
        decoder_kernel,
        out_shape=(out, out),
        in_specs=[sm] * 3 + [vm] * 8 + [hbm] * 6,
        out_specs=(vm, vm),
        scratch_shapes=[pltpu.VMEM((width, width), BF)] * 4
        + [pltpu.VMEM((width, units), BF)] * 2
        + [pltpu.VMEM((rows, width), BF)]
        + [pltpu.VMEM((2, width, BLK), BF)] * 3
        + [
            pltpu.VMEM((2 * chips, HD, BLK), BF),
            pltpu.VMEM((blocks, HD, BLK), BF),
            pltpu.VMEM((blocks, HD, BLK), BF),
            pltpu.VMEM((blocks * BLK, HD + blocks), BF),
            pltpu.VMEM((blocks, VROWS, BLK), BF),
            pltpu.VMEM((blocks // 4, HD + blocks, QN), BF),
            pltpu.VMEM((groups, VROWS, QN), F32),
            pltpu.VMEM((blocks, HD, HALF), F32),
            pltpu.VMEM((2 * chips, HD, BLK), BF),
            pltpu.VMEM((groups, keys, QN), F32),
            pltpu.VMEM((groups, keys, QN), F32),
            pltpu.VMEM((2, 2 * BLK, BLK), F32),
            pltpu.VMEM((2, chips, HD, BLK), BF),
            pltpu.VMEM((rows, width), F32),
            pltpu.VMEM((rows, width), BF),
            pltpu.VMEM((envs, per_env, width), BF),
            pltpu.VMEM((envs, per_env, units), F32),
            pltpu.VMEM((envs, per_env, units), F32),
            dma((6,)),
        ]
        + [dma((chips,))] * 4
        + [dma((2 * chips,))] * 2
        + [dma((chips,))] * 4
        + [dma((2 * chips,))] * 2
        + [dma((envs,))] * 2
        + [dma((5,))],
        compiler_params=pltpu.CompilerParams(
            collective_id=0, has_side_effects=True, vmem_limit_bytes=60 * 2**20
        ),
        name="decoder",
    )(
        rank, order, group_of_env, rank[None, :], visible, obs, actions, table, gain[None, :], w_head[None, :], returns,
        w_query, w_key, w_value, w_out, w_mix, w_group,
    )


def on_device(
    obs_rep, actions, action_table, decode_rank, visible, w_query, w_key, w_value, w_out,
    norm_gain, w_mix, w_group, w_head, returns, group_of_env,
):
    return decoder(
        decode_rank, group_of_env, visible, obs_rep[0], actions, action_table, norm_gain, w_head, returns,
        w_query, w_key, w_value, w_out, w_mix, w_group,
    )


def solution(mesh):
    spec = P(None, ("agent", "env"))
    in_specs = (P("env", "agent", None), P("env", "agent")) + (P(),) * 11 + (spec, P())
    return jax.shard_map(
        on_device, mesh=mesh, in_specs=in_specs, out_specs=(spec, spec), check_vma=False
    )
```

```python
import jax
import jax.numpy as jnp
import numpy as np
from jax import lax
from jax.experimental import pallas as pl
from jax.experimental.pallas import tpu as pltpu
from jax.sharding import PartitionSpec as P

H = 16
BLK = 128
HALF = BLK // 2
HD = 64
LOG2E = 1.4426950408889634
NEG = -1e30
VROWS = 80
QN = 256
SIDE = 4
MESH = pl.DeviceIdType.MESH
BF = jnp.bfloat16
F32 = jnp.float32


def agent_at(y, x, core):
    return (y * SIDE + x) * 2 + core


OFFSETS = (
    (0, 1), (0, 3), (1, 0), (3, 0), (0, 2), (2, 0), (1, 1), (3, 3),
    (1, 3), (3, 1), (1, 2), (3, 2), (2, 1), (2, 3), (2, 2),
)
EARLY = 8
RING = (1, 7, 2, 6, 3, 5, 4)


def pick(n, values):
    got = jnp.int32(values[0])
    for at, value in enumerate(values[1:], 1):
        got = jnp.where(n == at, value, got)
    return got


def chip_step(n):
    return pick(n, (0,) + tuple(y * SIDE + x for y, x in OFFSETS))


def decoder_kernel(
    rank_ref, order, group_ref, rank_row, visible_ref, obs_ref, act_ref, table_ref, gain_ref, whead_ref, ret_ref,
    wq_hbm, wk_hbm, wv_hbm, wo_hbm, wm_hbm, wg_hbm,
    val_ref, adv_ref,
    wq, wk, wv, wo, wm, wg, tok, kst, vst, qst, qbuf, kbuf, vbuf,
    ks, vs, qa, acc, osort, ost, sa, sb, pre, pre_peak, mask,
    att, resid, hid, hbuf, mix, part,
    load_sem, ks_send, ks_recv, vs_send, vs_recv, qs_send, qs_recv, kf_send, kf_recv, vf_send, vf_recv,
    a_send, a_recv, z_send, z_recv, local_sem, turn_sem,
):
    groups = acc.shape[0]
    env = lax.axis_index("env")
    envs = hbuf.shape[0]
    me = lax.axis_index("agent")
    core = lax.rem(me, 2)
    chip = me // 2
    my_y, my_x = chip // SIDE, lax.rem(chip, SIDE)
    chips = SIDE * SIDE
    sibling = chip * 2 + 1 - core
    pairs = ((wk_hbm, wk), (wq_hbm, wq), (wv_hbm, wv), (wo_hbm, wo), (wm_hbm, wm), (wg_hbm, wg))
    loads = [pltpu.make_async_copy(src, dst, load_sem.at[n]) for n, (src, dst) in enumerate(pairs)]
    for load in loads[:3]:
        load.start()
    barrier = pltpu.get_barrier_semaphore()

    def tell(step, _):
        other = lax.rem(me + step, 2 * chips)
        pl.semaphore_signal(barrier, inc=1, device_id={"agent": other}, device_id_type=MESH)
        return 0

    def tell_env(step, _):
        other = lax.rem(env + step, envs)
        pl.semaphore_signal(barrier, inc=1, device_id={"env": other}, device_id_type=MESH)
        return 0

    lax.fori_loop(1, 2 * chips, tell, 0)
    lax.fori_loop(1, envs, tell_env, 0)

    blocks = rank_row.shape[1]
    ids_r = lax.broadcasted_iota(jnp.int32, (blocks, blocks), 0)
    ids_c = lax.broadcasted_iota(jnp.int32, (blocks, blocks), 1)
    to_rank = (ids_r == rank_row[...]).astype(F32)

    onehot = (act_ref[...] == lax.broadcasted_iota(jnp.int32, (table_ref.shape[0], 2 * BLK), 0)).astype(F32)
    onehot = jnp.transpose(onehot).astype(BF)
    width = obs_ref.shape[1]
    strip = 256

    def embed(n, _):
        cols = pl.ds(pl.multiple_of(n * strip, strip), strip)
        added = jnp.dot(onehot, table_ref[:, cols], preferred_element_type=F32)
        tok[:, cols] = (obs_ref[:, cols].astype(F32) + added).astype(BF)
        return 0

    lax.fori_loop(0, width // strip, embed, 0)

    def project(rows, w, out):
        def one(n, _):
            cols = pl.ds(pl.multiple_of(n * strip, strip), strip)
            got = jnp.dot(rows, w[:, cols], preferred_element_type=F32).astype(BF)
            turned = jnp.transpose(got)
            out[0, cols, :] = turned[:, :BLK]
            out[1, cols, :] = turned[:, BLK:]
            return 0

        lax.fori_loop(0, width // strip, one, 0)

    def there(step):
        return lax.rem(my_y + step // SIDE, SIDE), lax.rem(my_x + lax.rem(step, SIDE), SIDE)

    def back(step):
        return lax.rem(my_y + SIDE - step // SIDE, SIDE), lax.rem(my_x + SIDE - lax.rem(step, SIDE), SIDE)

    def head_rows(y, x):
        return pl.ds(pl.multiple_of((y * SIDE + x) * HD, HD), HD)

    def send(stage, buf, sends, recvs, step):
        y, x = there(step)
        return pltpu.make_async_remote_copy(
            src_ref=stage.at[:, head_rows(y, x), :],
            dst_ref=buf.at[pl.ds(me * 2, 2)],
            send_sem=sends.at[step], recv_sem=recvs.at[step],
            device_id={"agent": agent_at(y, x, core)}, device_id_type=MESH,
        )

    def arrival(stage, buf, sends, recvs, step):
        y, x = back(step)
        return pltpu.make_async_remote_copy(
            src_ref=stage.at[:, head_rows(y, x), :],
            dst_ref=buf.at[pl.ds(agent_at(y, x, core) * 2, 2)],
            send_sem=sends.at[step], recv_sem=recvs.at[step],
            device_id={"agent": agent_at(y, x, core)}, device_id_type=MESH,
        )

    def own_forward(stage, buf, sends, recvs):
        return pltpu.make_async_remote_copy(
            src_ref=stage.at[:, head_rows(my_y, my_x), :],
            dst_ref=buf.at[pl.ds(me * 2, 2)],
            send_sem=sends.at[0], recv_sem=recvs.at[0],
            device_id={"agent": sibling}, device_id_type=MESH,
        )

    def forward(buf, sends, recvs, step):
        y, x = back(step)
        slot = pl.ds(agent_at(y, x, core) * 2, 2)
        return pltpu.make_async_remote_copy(
            src_ref=buf.at[slot], dst_ref=buf.at[slot],
            send_sem=sends.at[step], recv_sem=recvs.at[step],
            device_id={"agent": sibling}, device_id_type=MESH,
        )

    def forwarded(buf, sends, recvs, step):
        y, x = back(step)
        slot = pl.ds(agent_at(y, x, 1 - core) * 2, 2)
        return pltpu.make_async_remote_copy(
            src_ref=buf.at[slot], dst_ref=buf.at[slot],
            send_sem=sends.at[step], recv_sem=recvs.at[step],
            device_id={"agent": sibling}, device_id_type=MESH,
        )

    def local(stage, buf, n):
        return pltpu.make_async_copy(
            stage.at[:, head_rows(my_y, my_x), :], buf.at[pl.ds(me * 2, 2)], local_sem.at[n]
        )

    def send_all(stage, buf, sends, recvs, fsends, frecvs, n):
        local(stage, buf, n).start()
        own_forward(stage, buf, fsends, frecvs).start()

        def one(n, _):
            send(stage, buf, sends, recvs, chip_step(n)).start()
            return 0

        lax.fori_loop(1, chips, one, 0)

    def q_send(step, flip):
        y, x = there(step)
        target = lax.rem(core + flip, 2)
        return pltpu.make_async_remote_copy(
            src_ref=qst.at[target, head_rows(y, x), :],
            dst_ref=qbuf.at[me],
            send_sem=qs_send.at[flip * chips + step], recv_sem=qs_recv.at[flip * chips + step],
            device_id={"agent": agent_at(y, x, target)}, device_id_type=MESH,
        )

    def q_arrival(step, flip):
        y, x = back(step)
        source = agent_at(y, x, lax.rem(core + flip, 2))
        return pltpu.make_async_remote_copy(
            src_ref=qst.at[core, head_rows(y, x), :],
            dst_ref=qbuf.at[source],
            send_sem=qs_send.at[flip * chips + step], recv_sem=qs_recv.at[flip * chips + step],
            device_id={"agent": source}, device_id_type=MESH,
        )

    loads[0].wait()
    project(tok[...], wk, kst)
    pl.semaphore_wait(barrier, 2 * chips - 1 + envs - 1)
    for load in loads[3:]:
        load.start()
    send_all(kst, kbuf, ks_send, ks_recv, kf_send, kf_recv, 0)
    rows = jnp.concatenate(
        [obs_ref[0:HALF], obs_ref[BLK : BLK + HALF], obs_ref[HALF:BLK], obs_ref[BLK + HALF :]], axis=0
    )
    loads[1].wait()
    project(rows, wq, qst)
    q_local = pltpu.make_async_copy(qst.at[core, head_rows(my_y, my_x), :], qbuf.at[me], local_sem.at[2])
    q_local.start()
    q_send(0, 1).start()

    def q_one(n, _):
        step = chip_step(n)
        q_send(step, 0).start()
        q_send(step, 1).start()
        return 0

    lax.fori_loop(1, chips, q_one, 0)

    loads[2].wait()
    project(tok[...], wv, vst)
    send_all(vst, vbuf, vs_send, vs_recv, vf_send, vf_recv, 1)
    def pass_on(stage, buf, sends, recvs, fsends, frecvs):
        def one(n, _):
            step = chip_step(n)
            arrival(stage, buf, sends, recvs, step).wait_recv()
            forward(buf, fsends, frecvs, step).start()
            return 0

        def two(step, _):
            forwarded(buf, fsends, frecvs, step).wait_recv()
            return 0

        lax.fori_loop(1, chips, one, 0)
        lax.fori_loop(0, chips, two, 0)

    lane = lax.broadcasted_iota(jnp.int32, (BLK, HD), 1)
    row = lax.broadcasted_iota(jnp.int32, (VROWS - HD, BLK), 0)
    ones = jnp.where(row == 0, 1.0, 0.0).astype(BF)

    def prepare_keys(r, _):
        at = pl.multiple_of(r * BLK, BLK)
        hot = jnp.where(lane == r, 1.0, 0.0).astype(BF)
        ks[pl.ds(at, BLK), :] = jnp.concatenate([jnp.transpose(kbuf[order[r]]), hot], axis=1)
        return 0

    def prepare_values(r, _):
        vs[r] = jnp.concatenate([vbuf[order[r]], ones], axis=0)
        return 0

    to_rank = to_rank.astype(BF)
    vis = visible_ref[...].astype(F32).astype(BF)
    by_query = jnp.dot(to_rank, vis, preferred_element_type=F32).astype(BF)
    ranked = lax.dot_general(
        by_query, to_rank, (((1,), (1,)), ((), ())), preferred_element_type=F32
    )
    sees = ((ids_r > ids_c) & (ranked > 0.5)) | (ids_r == ids_c)
    sees = jnp.transpose(jnp.where(sees, 1.0, 0.0)).astype(BF)

    mrow = lax.broadcasted_iota(jnp.int32, (2 * BLK, BLK), 0)
    mcol = lax.broadcasted_iota(jnp.int32, (2 * BLK, BLK), 1)
    late = (mrow // BLK == mcol // HALF) & (lax.rem(mrow, BLK) > lax.rem(mcol, HALF) + core * HALF)
    mask[0] = jnp.zeros((2 * BLK, BLK), F32)
    mask[1] = jnp.where(late, NEG, 0.0)
    acc[...] = jnp.zeros_like(acc)

    qlane = lax.broadcasted_iota(jnp.int32, (HD, BLK), 1)
    spread_r = lax.broadcasted_iota(jnp.int32, (blocks, QN), 0)
    spread_c = lax.broadcasted_iota(jnp.int32, (blocks, QN), 1)

    def half(r, want):
        b = order[r]
        x = qbuf[b // 2].astype(F32)
        return jnp.where(jnp.full(x.shape, lax.rem(b, 2), jnp.int32) == want, x, pltpu.roll(x, HALF, 1))

    def prepare_queries(t, _):
        pieces = []
        for p in range(2):
            pieces.append(jnp.where(qlane < HALF, half(4 * t + 2 * p, 0), half(4 * t + 2 * p + 1, 1)))
        turned = (jnp.concatenate(pieces, axis=1) * HD**-0.5).astype(BF)
        spread = (spread_r == 4 * t + spread_c // HALF).astype(BF)
        open_ = jnp.dot(sees, spread, preferred_element_type=F32)
        bias = jnp.where(open_ > 0.5, 0.0, NEG).astype(BF)
        qa[t] = jnp.concatenate([turned, bias], axis=0)
        return 0

    per_tile = 4 * groups
    chunk_blocks = per_tile
    keys = chunk_blocks * BLK
    tiles = blocks // per_tile

    def place_of(i):
        p, j = i // (tiles + 1), lax.rem(i, tiles + 1)
        first = j < p + 1
        return jnp.where(first, p, tiles - 1 - p), jnp.where(first, j, j - p - 1)

    pass_on(kst, kbuf, ks_send, ks_recv, kf_send, kf_recv)
    local(kst, kbuf, 0).wait()
    lax.fori_loop(0, blocks, prepare_keys, 0, unroll=4)
    q_local.wait()
    q_arrival(0, 1).wait_recv()

    def q_land(step, _):
        q_arrival(step, 0).wait_recv()
        q_arrival(step, 1).wait_recv()
        return 0

    lax.fori_loop(1, chips, q_land, 0)
    lax.fori_loop(0, blocks // 4, prepare_queries, 0, unroll=2)

    def score(i, buf, which):
        t, c = place_of(i)
        diagonal = jnp.where(t == c, 1, 0)
        base = pl.multiple_of(c * keys, keys)
        peaks = []
        for g in which:
            full = jnp.dot(ks[pl.ds(base, keys), :], qa[t * groups + g], preferred_element_type=F32)
            peak = None
            for blk in range(0, chunk_blocks, 2):
                rows = full[blk * BLK : (blk + 2) * BLK]
                p = blk // 2 - 2 * g
                if 0 <= p < 2:
                    cols = [rows[:, :BLK], rows[:, BLK:]]
                    cols[p] = cols[p] + mask[diagonal]
                    rows = jnp.concatenate(cols, axis=1)
                buf[g, blk * BLK : (blk + 2) * BLK] = rows
                top = jnp.max(rows.reshape(2 * BLK // 8, 8, QN), axis=0)
                peak = top if peak is None else jnp.maximum(peak, top)
            peaks.append(jnp.max(peak, axis=0, keepdims=True))
        return tuple(peaks)

    def absorb(i, buf, peaks, running, which):
        t, c = place_of(i)
        new = []
        for g, peak, before in zip(which, peaks, running):
            old = jnp.where(jnp.full((1, QN), c, jnp.int32) == 0, NEG, before)
            top = jnp.maximum(old, peak)
            shrink = jnp.exp2((old - top) * LOG2E)
            expo = jnp.exp2((buf[g] - top) * LOG2E).astype(BF)
            vals = jnp.concatenate([vs[c * chunk_blocks + j] for j in range(chunk_blocks)], axis=1)
            acc[g] = acc[g] * shrink + jnp.dot(vals, expo, preferred_element_type=F32)
            new.append(top)

        return tuple(new)

    def finish_tile(i):
        t, c = place_of(i)

        @pl.when(c == t)
        def _():
            for g in range(groups):
                a = acc[g]
                out = a[:HD] / a[HD : HD + 1]
                for j in range(4):
                    osort[t * per_tile + g * 4 + j] = out[:, j * HALF : (j + 1) * HALF]

    def both(i, now, later, peaks, running):
        next_peaks, next_running = (), ()
        for g in range(groups):
            next_peaks += score(i + 1, later, (g,))
            next_running += absorb(i, now, peaks[g : g + 1], running[g : g + 1], (g,))
        finish_tile(i)
        return next_peaks, next_running

    def two(h, carry):
        peaks, running = both(2 * h, sa, sb, *carry)
        return both(2 * h + 1, sb, sa, peaks, running)

    early = pre.shape[0]

    def score_early(i, _):
        for g, peak in enumerate(score(i, pre.at[i], range(groups))):
            pre_peak[i, g : g + 1] = peak
        return 0

    lax.fori_loop(0, early, score_early, 0)
    pass_on(vst, vbuf, vs_send, vs_recv, vf_send, vf_recv)
    local(vst, vbuf, 1).wait()
    lax.fori_loop(0, blocks, prepare_values, 0, unroll=4)

    def absorb_early(i, running):
        new = ()
        for g in range(groups):
            new += absorb(i, pre.at[i], (pre_peak[i, g : g + 1],), running[g : g + 1], (g,))
        finish_tile(i)
        return new

    running = tuple(jnp.full((1, QN), NEG, F32) for _ in range(groups))
    running = lax.fori_loop(0, early, absorb_early, running)
    steps = tiles * (tiles + 1) // 2
    lax.fori_loop(early // 2, steps // 2, two, (score(early, sa, range(groups)), running))

    def o_send(step, flip):
        y = lax.rem(my_y + step // SIDE, SIDE)
        x = lax.rem(my_x + lax.rem(step, SIDE), SIDE)
        target = agent_at(y, x, lax.rem(core + flip, 2))
        return pltpu.make_async_remote_copy(
            src_ref=ost.at[target], dst_ref=att.at[core, chip],
            send_sem=a_send.at[flip * chips + step], recv_sem=a_recv.at[flip * chips + step],
            device_id={"agent": target}, device_id_type=MESH,
        )

    def o_arrival(step, flip):
        y = lax.rem(my_y + SIDE - step // SIDE, SIDE)
        x = lax.rem(my_x + SIDE - lax.rem(step, SIDE), SIDE)
        other = lax.rem(core + flip, 2)
        return pltpu.make_async_remote_copy(
            src_ref=ost.at[me], dst_ref=att.at[other, y * SIDE + x],
            send_sem=a_send.at[flip * chips + step], recv_sem=a_recv.at[flip * chips + step],
            device_id={"agent": agent_at(y, x, other)}, device_id_type=MESH,
        )

    def unsort(target):
        pair = [osort[rank_ref[2 * target]], osort[rank_ref[2 * target + 1]]]
        ost[target] = jnp.concatenate(pair, axis=1).astype(BF)

    own = pltpu.make_async_copy(ost.at[me], att.at[core, chip], local_sem.at[3])

    def start(n, _):
        step = chip_step(n)
        o_send(step, 0).start()
        o_send(step, 1).start()
        return 0

    def sent(step, _):
        o_send(step, 0).wait_send()
        o_send(step, 1).wait_send()
        return 0

    def unsort_all(a, _):
        unsort(a)
        return 0

    def start_all():
        o_send(0, 1).start()
        own.start()
        lax.fori_loop(1, chips, start, 0)

    def sent_all():
        o_send(0, 1).wait_send()
        lax.fori_loop(1, chips, sent, 0)

    lax.fori_loop(0, 2 * chips, unsort_all, 0, unroll=2)

    @pl.when(core == 0)
    def _():
        start_all()
        sent_all()
        pl.semaphore_signal(turn_sem, inc=1, device_id={"agent": sibling}, device_id_type=MESH)

    @pl.when(core == 1)
    def _():
        pl.semaphore_wait(turn_sem, 1)
        start_all()

    def land_from(which):
        flip = jnp.where(core == which, 0, 1)

        @pl.when(core == which)
        def _():
            own.wait()

        @pl.when(core != which)
        def _():
            o_arrival(0, 1).wait_recv()

        def land(step, _):
            o_arrival(step, flip).wait_recv()
            return 0

        lax.fori_loop(1, chips, land, 0)

    wide = 256
    per_env = 2 * BLK // envs

    def piece(e):
        quarter = lax.rem(e, 4)
        return pl.ds(pl.multiple_of(quarter // 2 * BLK + e // 4 * HALF + lax.rem(quarter, 2) * per_env, per_env), per_env)

    def z_copy(step):
        other = lax.rem(env + step, envs)
        return pltpu.make_async_remote_copy(
            src_ref=hid.at[piece(other)], dst_ref=hbuf.at[env],
            send_sem=z_send.at[step], recv_sem=z_recv.at[step],
            device_id={"env": other}, device_id_type=MESH,
        )

    def z_arrival(step):
        other = lax.rem(env + envs - step, envs)
        return pltpu.make_async_remote_copy(
            src_ref=hid.at[piece(env)], dst_ref=hbuf.at[other],
            send_sem=z_send.at[step], recv_sem=z_recv.at[step],
            device_id={"env": other}, device_id_type=MESH,
        )

    mine = pltpu.make_async_copy(hid.at[piece(env)], hbuf.at[env], local_sem.at[4])
    loads[3].wait()
    for half in range(2):
        land_from(half)
        turned = jnp.transpose(att[half].reshape(width, BLK))
        seen = jnp.concatenate(
            [obs_ref[half * HALF : (half + 1) * HALF], obs_ref[BLK + half * HALF : BLK + (half + 1) * HALF]], axis=0
        ).astype(F32)
        for n in range(width // wide):
            cols = slice(n * wide, (n + 1) * wide)
            resid[half * BLK : (half + 1) * BLK, cols] = seen[:, cols] + jnp.dot(
                turned, wo[:, cols], preferred_element_type=F32
            )
        whole = resid[half * BLK : (half + 1) * BLK, :]
        factor = lax.rsqrt(jnp.mean(whole * whole, axis=1, keepdims=True) + 1e-05)
        hid[half * BLK : (half + 1) * BLK, :] = (whole * factor * gain_ref[...]).astype(BF)

        def z_start(n, _):
            step = pick(n, (0,) + RING)

            @pl.when(lax.rem(lax.rem(env + step, envs), 4) // 2 == half)
            def _():
                z_copy(step).start()

            return 0

        lax.fori_loop(1, envs, z_start, 0)
    mine.start()
    loads[4].wait()
    loads[5].wait()
    mine.wait()
    for together in ((0, 1, 7), (2, 6), (3, 5, 4)):
        for step in together:
            if step:
                z_arrival(step).wait_recv()
        places = [lax.rem(env + envs - step, envs) for step in together]
        moved = jnp.concatenate([hbuf[at] for at in places], axis=0)
        for n in range(whead_ref.shape[1] // wide):
            cols = slice(n * wide, (n + 1) * wide)
            mixed = jnp.dot(moved, wm[:, cols], preferred_element_type=F32)
            parted = jnp.dot(moved, wg[:, cols], preferred_element_type=F32)
            for m, at in enumerate(places):
                mix[at, :, cols] = mixed[m * per_env : (m + 1) * per_env]
                part[at, :, cols] = parted[m * per_env : (m + 1) * per_env]
    partners = []
    values = []
    for e in range(envs):
        partner = jnp.int32(0)
        for f in range(envs):
            if f != e:
                partner = jnp.where(group_ref[f] == group_ref[e], f, partner)
        partners.append(partner)
        x = mix[e] + 0.5 * (part[e] + part[partner])
        activ = 0.5 * x * (1.0 + lax.erf(x * np.float32(np.sqrt(0.5))))
        values.append(jnp.sum(activ * whead_ref[...], axis=1, keepdims=True).T)
    for e in range(envs):
        val_ref[e : e + 1, :] = values[e]
    excess = ret_ref[...] - val_ref[...]
    rows = lax.broadcasted_iota(jnp.int32, (envs, per_env), 0)
    for e in range(envs):
        mine_ = excess[e : e + 1]
        other = jnp.sum(jnp.where(rows == jnp.full(rows.shape, partners[e], jnp.int32), excess, 0.0), axis=0, keepdims=True)
        adv_ref[e : e + 1, :] = mine_ - 0.5 * (mine_ + other)

    own_forward(kst, kbuf, kf_send, kf_recv).wait_send()
    own_forward(vst, vbuf, vf_send, vf_recv).wait_send()
    q_send(0, 1).wait_send()

    @pl.when(core == 1)
    def _():
        sent_all()

    def finish(step, _):
        send(kst, kbuf, ks_send, ks_recv, step).wait_send()
        send(vst, vbuf, vs_send, vs_recv, step).wait_send()
        forward(kbuf, kf_send, kf_recv, step).wait_send()
        forward(vbuf, vf_send, vf_recv, step).wait_send()
        for flip in range(2):
            q_send(step, flip).wait_send()
        return 0

    lax.fori_loop(1, chips, finish, 0)

    def z_finish(step, _):
        z_copy(step).wait_send()
        return 0

    lax.fori_loop(1, envs, z_finish, 0)


def decoder(rank, group_of_env, visible, obs, actions, table, gain, w_head, returns, w_query, w_key, w_value, w_out, w_mix, w_group):
    rows, width = obs.shape
    envs, per_env = returns.shape
    units = w_head.shape[0]
    blocks = rank.shape[0]
    chips = SIDE * SIDE
    groups = 2
    keys = 4 * groups * BLK
    ids = jnp.arange(blocks, dtype=jnp.int32)
    order = jnp.sum(jnp.where(rank[None, :] == ids[:, None], ids[None, :], 0), axis=1)
    sm = pl.BlockSpec(memory_space=pltpu.SMEM)
    vm = pl.BlockSpec(memory_space=pltpu.VMEM)
    hbm = pl.BlockSpec(memory_space=pl.ANY)
    dma = pltpu.SemaphoreType.DMA
    out = jax.ShapeDtypeStruct((envs, per_env), F32)
    return pl.pallas_call(
        decoder_kernel,
        out_shape=(out, out),
        in_specs=[sm] * 3 + [vm] * 8 + [hbm] * 6,
        out_specs=(vm, vm),
        scratch_shapes=[pltpu.VMEM((width, width), BF)] * 4
        + [pltpu.VMEM((width, units), BF)] * 2
        + [pltpu.VMEM((rows, width), BF)]
        + [pltpu.VMEM((2, width, BLK), BF)] * 3
        + [
            pltpu.VMEM((2 * chips, HD, BLK), BF),
            pltpu.VMEM((blocks, HD, BLK), BF),
            pltpu.VMEM((blocks, HD, BLK), BF),
            pltpu.VMEM((blocks * BLK, HD + blocks), BF),
            pltpu.VMEM((blocks, VROWS, BLK), BF),
            pltpu.VMEM((blocks // 4, HD + blocks, QN), BF),
            pltpu.VMEM((groups, VROWS, QN), F32),
            pltpu.VMEM((blocks, HD, HALF), F32),
            pltpu.VMEM((2 * chips, HD, BLK), BF),
            pltpu.VMEM((groups, keys, QN), F32),
            pltpu.VMEM((groups, keys, QN), F32),
            pltpu.VMEM((EARLY, groups, keys, QN), F32),
            pltpu.VMEM((EARLY, 8, QN), F32),
            pltpu.VMEM((2, 2 * BLK, BLK), F32),
            pltpu.VMEM((2, chips, HD, BLK), BF),
            pltpu.VMEM((rows, width), F32),
            pltpu.VMEM((rows, width), BF),
            pltpu.VMEM((envs, per_env, width), BF),
            pltpu.VMEM((envs, per_env, units), F32),
            pltpu.VMEM((envs, per_env, units), F32),
            dma((6,)),
        ]
        + [dma((chips,))] * 4
        + [dma((2 * chips,))] * 2
        + [dma((chips,))] * 4
        + [dma((2 * chips,))] * 2
        + [dma((envs,))] * 2
        + [dma((5,)), pltpu.SemaphoreType.REGULAR],
        compiler_params=pltpu.CompilerParams(
            collective_id=0, has_side_effects=True, vmem_limit_bytes=60 * 2**20
        ),
        name="decoder",
    )(
        rank, order, group_of_env, rank[None, :], visible, obs, actions, table, gain[None, :], w_head[None, :], returns,
        w_query, w_key, w_value, w_out, w_mix, w_group,
    )


def on_device(
    obs_rep, actions, action_table, decode_rank, visible, w_query, w_key, w_value, w_out,
    norm_gain, w_mix, w_group, w_head, returns, group_of_env,
):
    return decoder(
        decode_rank, group_of_env, visible, obs_rep[0], actions, action_table, norm_gain, w_head, returns,
        w_query, w_key, w_value, w_out, w_mix, w_group,
    )


def solution(mesh):
    spec = P(None, ("agent", "env"))
    in_specs = (P("env", "agent", None), P("env", "agent")) + (P(),) * 11 + (spec, P())
    return jax.shard_map(
        on_device, mesh=mesh, in_specs=in_specs, out_specs=(spec, spec), check_vma=False
    )
```

```python
import jax
import jax.numpy as jnp
import numpy as np
from jax import lax
from jax.experimental import pallas as pl
from jax.experimental.pallas import tpu as pltpu
from jax.sharding import PartitionSpec as P

H = 16
BLK = 128
HALF = BLK // 2
HD = 64
LOG2E = 1.4426950408889634
NEG = -1e30
VROWS = 80
QN = 256
SIDE = 4
MESH = pl.DeviceIdType.MESH
BF = jnp.bfloat16
F32 = jnp.float32


def agent_at(y, x, core):
    return (y * SIDE + x) * 2 + core


OFFSETS = (
    (0, 1), (0, 3), (1, 0), (3, 0), (0, 2), (2, 0), (1, 1), (3, 3),
    (1, 3), (3, 1), (1, 2), (3, 2), (2, 1), (2, 3), (2, 2),
)
EARLY = 8
RING = (1, 7, 2, 6, 3, 5, 4)


def pick(n, values):
    got = jnp.int32(values[0])
    for at, value in enumerate(values[1:], 1):
        got = jnp.where(n == at, value, got)
    return got


def chip_step(n):
    return pick(n, (0,) + tuple(y * SIDE + x for y, x in OFFSETS))


def decoder_kernel(
    rank_ref, order, group_ref, rank_row, visible_ref, act_ref, table_ref, gain_ref, whead_ref, ret_ref,
    obs_hbm, wq_hbm, wk_hbm, wv_hbm, wo_hbm, wm_hbm, wg_hbm,
    val_ref, adv_ref,
    obs_ref, wq, wk, wv, wo, wm, wg, tok, kst, vst, qst, qbuf, kbuf, vbuf,
    ks, vs, qa, acc, osort, ost, sa, sb, pre, pre_peak, mask,
    att, resid, hid, hbuf, mix, part,
    load_sem, ks_send, ks_recv, vs_send, vs_recv, qs_send, qs_recv, kf_send, kf_recv, vf_send, vf_recv,
    a_send, a_recv, z_send, z_recv, local_sem, turn_sem,
):
    groups = acc.shape[0]
    env = lax.axis_index("env")
    envs = hbuf.shape[0]
    me = lax.axis_index("agent")
    core = lax.rem(me, 2)
    chip = me // 2
    my_y, my_x = chip // SIDE, lax.rem(chip, SIDE)
    chips = SIDE * SIDE
    sibling = chip * 2 + 1 - core
    obs_load = pltpu.make_async_copy(obs_hbm, obs_ref, local_sem.at[5])
    obs_load.start()
    pairs = ((wk_hbm, wk), (wq_hbm, wq), (wv_hbm, wv), (wo_hbm, wo), (wm_hbm, wm), (wg_hbm, wg))
    loads = [pltpu.make_async_copy(src, dst, load_sem.at[n]) for n, (src, dst) in enumerate(pairs)]
    for load in loads[:3]:
        load.start()
    barrier = pltpu.get_barrier_semaphore()

    def tell(step, _):
        other = lax.rem(me + step, 2 * chips)
        pl.semaphore_signal(barrier, inc=1, device_id={"agent": other}, device_id_type=MESH)
        return 0

    def tell_env(step, _):
        other = lax.rem(env + step, envs)
        pl.semaphore_signal(barrier, inc=1, device_id={"env": other}, device_id_type=MESH)
        return 0

    lax.fori_loop(1, 2 * chips, tell, 0)
    lax.fori_loop(1, envs, tell_env, 0)

    blocks = rank_row.shape[1]
    ids_r = lax.broadcasted_iota(jnp.int32, (blocks, blocks), 0)
    ids_c = lax.broadcasted_iota(jnp.int32, (blocks, blocks), 1)
    to_rank = (ids_r == rank_row[...]).astype(F32)

    onehot = (act_ref[...] == lax.broadcasted_iota(jnp.int32, (table_ref.shape[0], 2 * BLK), 0)).astype(F32)
    onehot = jnp.transpose(onehot).astype(BF)
    width = obs_ref.shape[1]
    strip = 256

    def embed(n, _):
        cols = pl.ds(pl.multiple_of(n * strip, strip), strip)
        added = jnp.dot(onehot, table_ref[:, cols], preferred_element_type=F32)
        tok[:, cols] = (obs_ref[:, cols].astype(F32) + added).astype(BF)
        return 0

    obs_load.wait()
    lax.fori_loop(0, width // strip, embed, 0)

    def project(rows, w, out):
        def one(n, _):
            cols = pl.ds(pl.multiple_of(n * strip, strip), strip)
            got = jnp.dot(rows, w[:, cols], preferred_element_type=F32).astype(BF)
            turned = jnp.transpose(got)
            out[0, cols, :] = turned[:, :BLK]
            out[1, cols, :] = turned[:, BLK:]
            return 0

        lax.fori_loop(0, width // strip, one, 0)

    def there(step):
        return lax.rem(my_y + step // SIDE, SIDE), lax.rem(my_x + lax.rem(step, SIDE), SIDE)

    def back(step):
        return lax.rem(my_y + SIDE - step // SIDE, SIDE), lax.rem(my_x + SIDE - lax.rem(step, SIDE), SIDE)

    def head_rows(y, x):
        return pl.ds(pl.multiple_of((y * SIDE + x) * HD, HD), HD)

    def send(stage, buf, sends, recvs, step):
        y, x = there(step)
        return pltpu.make_async_remote_copy(
            src_ref=stage.at[:, head_rows(y, x), :],
            dst_ref=buf.at[pl.ds(me * 2, 2)],
            send_sem=sends.at[step], recv_sem=recvs.at[step],
            device_id={"agent": agent_at(y, x, core)}, device_id_type=MESH,
        )

    def arrival(stage, buf, sends, recvs, step):
        y, x = back(step)
        return pltpu.make_async_remote_copy(
            src_ref=stage.at[:, head_rows(y, x), :],
            dst_ref=buf.at[pl.ds(agent_at(y, x, core) * 2, 2)],
            send_sem=sends.at[step], recv_sem=recvs.at[step],
            device_id={"agent": agent_at(y, x, core)}, device_id_type=MESH,
        )

    def own_forward(stage, buf, sends, recvs):
        return pltpu.make_async_remote_copy(
            src_ref=stage.at[:, head_rows(my_y, my_x), :],
            dst_ref=buf.at[pl.ds(me * 2, 2)],
            send_sem=sends.at[0], recv_sem=recvs.at[0],
            device_id={"agent": sibling}, device_id_type=MESH,
        )

    def forward(buf, sends, recvs, step):
        y, x = back(step)
        slot = pl.ds(agent_at(y, x, core) * 2, 2)
        return pltpu.make_async_remote_copy(
            src_ref=buf.at[slot], dst_ref=buf.at[slot],
            send_sem=sends.at[step], recv_sem=recvs.at[step],
            device_id={"agent": sibling}, device_id_type=MESH,
        )

    def forwarded(buf, sends, recvs, step):
        y, x = back(step)
        slot = pl.ds(agent_at(y, x, 1 - core) * 2, 2)
        return pltpu.make_async_remote_copy(
            src_ref=buf.at[slot], dst_ref=buf.at[slot],
            send_sem=sends.at[step], recv_sem=recvs.at[step],
            device_id={"agent": sibling}, device_id_type=MESH,
        )

    def local(stage, buf, n):
        return pltpu.make_async_copy(
            stage.at[:, head_rows(my_y, my_x), :], buf.at[pl.ds(me * 2, 2)], local_sem.at[n]
        )

    def send_all(stage, buf, sends, recvs, fsends, frecvs, n):
        local(stage, buf, n).start()
        own_forward(stage, buf, fsends, frecvs).start()

        def one(n, _):
            send(stage, buf, sends, recvs, chip_step(n)).start()
            return 0

        lax.fori_loop(1, chips, one, 0)

    def q_send(step, flip):
        y, x = there(step)
        target = lax.rem(core + flip, 2)
        return pltpu.make_async_remote_copy(
            src_ref=qst.at[target, head_rows(y, x), :],
            dst_ref=qbuf.at[me],
            send_sem=qs_send.at[flip * chips + step], recv_sem=qs_recv.at[flip * chips + step],
            device_id={"agent": agent_at(y, x, target)}, device_id_type=MESH,
        )

    def q_arrival(step, flip):
        y, x = back(step)
        source = agent_at(y, x, lax.rem(core + flip, 2))
        return pltpu.make_async_remote_copy(
            src_ref=qst.at[core, head_rows(y, x), :],
            dst_ref=qbuf.at[source],
            send_sem=qs_send.at[flip * chips + step], recv_sem=qs_recv.at[flip * chips + step],
            device_id={"agent": source}, device_id_type=MESH,
        )

    loads[0].wait()
    project(tok[...], wk, kst)
    pl.semaphore_wait(barrier, 2 * chips - 1 + envs - 1)
    for load in loads[3:]:
        load.start()
    send_all(kst, kbuf, ks_send, ks_recv, kf_send, kf_recv, 0)
    rows = jnp.concatenate(
        [obs_ref[0:HALF], obs_ref[BLK : BLK + HALF], obs_ref[HALF:BLK], obs_ref[BLK + HALF :]], axis=0
    )
    loads[1].wait()
    project(rows, wq, qst)
    q_local = pltpu.make_async_copy(qst.at[core, head_rows(my_y, my_x), :], qbuf.at[me], local_sem.at[2])
    q_local.start()
    q_send(0, 1).start()

    def q_one(n, _):
        step = chip_step(n)
        q_send(step, 0).start()
        q_send(step, 1).start()
        return 0

    lax.fori_loop(1, chips, q_one, 0)

    loads[2].wait()
    project(tok[...], wv, vst)
    send_all(vst, vbuf, vs_send, vs_recv, vf_send, vf_recv, 1)
    def pass_on(stage, buf, sends, recvs, fsends, frecvs):
        def one(n, _):
            step = chip_step(n)
            arrival(stage, buf, sends, recvs, step).wait_recv()
            forward(buf, fsends, frecvs, step).start()
            return 0

        def two(step, _):
            forwarded(buf, fsends, frecvs, step).wait_recv()
            return 0

        lax.fori_loop(1, chips, one, 0)
        lax.fori_loop(0, chips, two, 0)

    lane = lax.broadcasted_iota(jnp.int32, (BLK, HD), 1)
    row = lax.broadcasted_iota(jnp.int32, (VROWS - HD, BLK), 0)
    ones = jnp.where(row == 0, 1.0, 0.0).astype(BF)

    def prepare_keys(r, _):
        at = pl.multiple_of(r * BLK, BLK)
        hot = jnp.where(lane == r, 1.0, 0.0).astype(BF)
        ks[pl.ds(at, BLK), :] = jnp.concatenate([jnp.transpose(kbuf[order[r]]), hot], axis=1)
        return 0

    def prepare_values(r, _):
        vs[r] = jnp.concatenate([vbuf[order[r]], ones], axis=0)
        return 0

    to_rank = to_rank.astype(BF)
    vis = visible_ref[...].astype(F32).astype(BF)
    by_query = jnp.dot(to_rank, vis, preferred_element_type=F32).astype(BF)
    ranked = lax.dot_general(
        by_query, to_rank, (((1,), (1,)), ((), ())), preferred_element_type=F32
    )
    sees = ((ids_r > ids_c) & (ranked > 0.5)) | (ids_r == ids_c)
    sees = jnp.transpose(jnp.where(sees, 1.0, 0.0)).astype(BF)

    mrow = lax.broadcasted_iota(jnp.int32, (2 * BLK, BLK), 0)
    mcol = lax.broadcasted_iota(jnp.int32, (2 * BLK, BLK), 1)
    late = (mrow // BLK == mcol // HALF) & (lax.rem(mrow, BLK) > lax.rem(mcol, HALF) + core * HALF)
    mask[0] = jnp.zeros((2 * BLK, BLK), F32)
    mask[1] = jnp.where(late, NEG, 0.0)
    acc[...] = jnp.zeros_like(acc)

    qlane = lax.broadcasted_iota(jnp.int32, (HD, BLK), 1)
    spread_r = lax.broadcasted_iota(jnp.int32, (blocks, QN), 0)
    spread_c = lax.broadcasted_iota(jnp.int32, (blocks, QN), 1)

    def half(r, want):
        b = order[r]
        x = qbuf[b // 2].astype(F32)
        return jnp.where(jnp.full(x.shape, lax.rem(b, 2), jnp.int32) == want, x, pltpu.roll(x, HALF, 1))

    def prepare_queries(t, _):
        pieces = []
        for p in range(2):
            pieces.append(jnp.where(qlane < HALF, half(4 * t + 2 * p, 0), half(4 * t + 2 * p + 1, 1)))
        turned = (jnp.concatenate(pieces, axis=1) * HD**-0.5).astype(BF)
        spread = (spread_r == 4 * t + spread_c // HALF).astype(BF)
        open_ = jnp.dot(sees, spread, preferred_element_type=F32)
        bias = jnp.where(open_ > 0.5, 0.0, NEG).astype(BF)
        qa[t] = jnp.concatenate([turned, bias], axis=0)
        return 0

    per_tile = 4 * groups
    chunk_blocks = per_tile
    keys = chunk_blocks * BLK
    tiles = blocks // per_tile

    def place_of(i):
        p, j = i // (tiles + 1), lax.rem(i, tiles + 1)
        first = j < p + 1
        return jnp.where(first, p, tiles - 1 - p), jnp.where(first, j, j - p - 1)

    pass_on(kst, kbuf, ks_send, ks_recv, kf_send, kf_recv)
    local(kst, kbuf, 0).wait()
    lax.fori_loop(0, blocks, prepare_keys, 0, unroll=4)
    q_local.wait()
    q_arrival(0, 1).wait_recv()

    def q_land(step, _):
        q_arrival(step, 0).wait_recv()
        q_arrival(step, 1).wait_recv()
        return 0

    lax.fori_loop(1, chips, q_land, 0)
    lax.fori_loop(0, blocks // 4, prepare_queries, 0, unroll=2)

    def score(i, buf, which):
        t, c = place_of(i)
        diagonal = jnp.where(t == c, 1, 0)
        base = pl.multiple_of(c * keys, keys)
        peaks = []
        for g in which:
            full = jnp.dot(ks[pl.ds(base, keys), :], qa[t * groups + g], preferred_element_type=F32)
            peak = None
            for blk in range(0, chunk_blocks, 2):
                rows = full[blk * BLK : (blk + 2) * BLK]
                p = blk // 2 - 2 * g
                if 0 <= p < 2:
                    cols = [rows[:, :BLK], rows[:, BLK:]]
                    cols[p] = cols[p] + mask[diagonal]
                    rows = jnp.concatenate(cols, axis=1)
                buf[g, blk * BLK : (blk + 2) * BLK] = rows
                top = jnp.max(rows.reshape(2 * BLK // 8, 8, QN), axis=0)
                peak = top if peak is None else jnp.maximum(peak, top)
            peaks.append(jnp.max(peak, axis=0, keepdims=True))
        return tuple(peaks)

    def absorb(i, buf, peaks, running, which):
        t, c = place_of(i)
        new = []
        for g, peak, before in zip(which, peaks, running):
            old = jnp.where(jnp.full((1, QN), c, jnp.int32) == 0, NEG, before)
            top = jnp.maximum(old, peak)
            shrink = jnp.exp2((old - top) * LOG2E)
            expo = jnp.exp2((buf[g] - top) * LOG2E).astype(BF)
            vals = jnp.concatenate([vs[c * chunk_blocks + j] for j in range(chunk_blocks)], axis=1)
            acc[g] = acc[g] * shrink + jnp.dot(vals, expo, preferred_element_type=F32)
            new.append(top)

        return tuple(new)

    def finish_tile(i):
        t, c = place_of(i)

        @pl.when(c == t)
        def _():
            for g in range(groups):
                a = acc[g]
                out = a[:HD] / a[HD : HD + 1]
                for j in range(4):
                    osort[t * per_tile + g * 4 + j] = out[:, j * HALF : (j + 1) * HALF]

    def both(i, now, later, peaks, running):
        next_peaks, next_running = (), ()
        for g in range(groups):
            next_peaks += score(i + 1, later, (g,))
            next_running += absorb(i, now, peaks[g : g + 1], running[g : g + 1], (g,))
        finish_tile(i)
        return next_peaks, next_running

    def two(h, carry):
        peaks, running = both(2 * h, sa, sb, *carry)
        return both(2 * h + 1, sb, sa, peaks, running)

    early = pre.shape[0]

    def score_early(i, _):
        for g, peak in enumerate(score(i, pre.at[i], range(groups))):
            pre_peak[i, g : g + 1] = peak
        return 0

    lax.fori_loop(0, early, score_early, 0)
    pass_on(vst, vbuf, vs_send, vs_recv, vf_send, vf_recv)
    local(vst, vbuf, 1).wait()
    lax.fori_loop(0, blocks, prepare_values, 0, unroll=4)

    def absorb_early(i, running):
        new = ()
        for g in range(groups):
            new += absorb(i, pre.at[i], (pre_peak[i, g : g + 1],), running[g : g + 1], (g,))
        finish_tile(i)
        return new

    running = tuple(jnp.full((1, QN), NEG, F32) for _ in range(groups))
    running = lax.fori_loop(0, early, absorb_early, running)
    steps = tiles * (tiles + 1) // 2
    lax.fori_loop(early // 2, steps // 2, two, (score(early, sa, range(groups)), running))

    def o_send(step, flip):
        y = lax.rem(my_y + step // SIDE, SIDE)
        x = lax.rem(my_x + lax.rem(step, SIDE), SIDE)
        target = agent_at(y, x, lax.rem(core + flip, 2))
        return pltpu.make_async_remote_copy(
            src_ref=ost.at[target], dst_ref=att.at[core, chip],
            send_sem=a_send.at[flip * chips + step], recv_sem=a_recv.at[flip * chips + step],
            device_id={"agent": target}, device_id_type=MESH,
        )

    def o_arrival(step, flip):
        y = lax.rem(my_y + SIDE - step // SIDE, SIDE)
        x = lax.rem(my_x + SIDE - lax.rem(step, SIDE), SIDE)
        other = lax.rem(core + flip, 2)
        return pltpu.make_async_remote_copy(
            src_ref=ost.at[me], dst_ref=att.at[other, y * SIDE + x],
            send_sem=a_send.at[flip * chips + step], recv_sem=a_recv.at[flip * chips + step],
            device_id={"agent": agent_at(y, x, other)}, device_id_type=MESH,
        )

    def unsort(target):
        pair = [osort[rank_ref[2 * target]], osort[rank_ref[2 * target + 1]]]
        ost[target] = jnp.concatenate(pair, axis=1).astype(BF)

    own = pltpu.make_async_copy(ost.at[me], att.at[core, chip], local_sem.at[3])

    def start(n, _):
        step = chip_step(n)
        o_send(step, 0).start()
        o_send(step, 1).start()
        return 0

    def sent(step, _):
        o_send(step, 0).wait_send()
        o_send(step, 1).wait_send()
        return 0

    def unsort_all(a, _):
        unsort(a)
        return 0

    def start_all():
        o_send(0, 1).start()
        own.start()
        lax.fori_loop(1, chips, start, 0)

    def sent_all():
        o_send(0, 1).wait_send()
        lax.fori_loop(1, chips, sent, 0)

    def place_and_start(n, _):
        step = chip_step(n)
        y, x = there(step)
        unsort(agent_at(y, x, 0))
        unsort(agent_at(y, x, 1))
        o_send(step, 0).start()
        o_send(step, 1).start()
        return 0

    @pl.when(core == 0)
    def _():
        lax.fori_loop(1, chips, place_and_start, 0)
        unsort(sibling)
        unsort(me)
        o_send(0, 1).start()
        own.start()
        sent_all()
        pl.semaphore_signal(turn_sem, inc=1, device_id={"agent": sibling}, device_id_type=MESH)

    @pl.when(core == 1)
    def _():
        lax.fori_loop(0, 2 * chips, unsort_all, 0, unroll=2)
        pl.semaphore_wait(turn_sem, 1)
        start_all()

    def land_from(which):
        flip = jnp.where(core == which, 0, 1)

        @pl.when(core == which)
        def _():
            own.wait()

        @pl.when(core != which)
        def _():
            o_arrival(0, 1).wait_recv()

        def land(step, _):
            o_arrival(step, flip).wait_recv()
            return 0

        lax.fori_loop(1, chips, land, 0)

    wide = 256
    per_env = 2 * BLK // envs

    def piece(e):
        quarter = lax.rem(e, 4)
        return pl.ds(pl.multiple_of(quarter // 2 * BLK + e // 4 * HALF + lax.rem(quarter, 2) * per_env, per_env), per_env)

    def z_copy(step):
        other = lax.rem(env + step, envs)
        return pltpu.make_async_remote_copy(
            src_ref=hid.at[piece(other)], dst_ref=hbuf.at[env],
            send_sem=z_send.at[step], recv_sem=z_recv.at[step],
            device_id={"env": other}, device_id_type=MESH,
        )

    def z_arrival(step):
        other = lax.rem(env + envs - step, envs)
        return pltpu.make_async_remote_copy(
            src_ref=hid.at[piece(env)], dst_ref=hbuf.at[other],
            send_sem=z_send.at[step], recv_sem=z_recv.at[step],
            device_id={"env": other}, device_id_type=MESH,
        )

    mine = pltpu.make_async_copy(hid.at[piece(env)], hbuf.at[env], local_sem.at[4])
    loads[3].wait()
    for half in range(2):
        land_from(half)
        turned = jnp.transpose(att[half].reshape(width, BLK))
        seen = jnp.concatenate(
            [obs_ref[half * HALF : (half + 1) * HALF], obs_ref[BLK + half * HALF : BLK + (half + 1) * HALF]], axis=0
        ).astype(F32)
        for n in range(width // wide):
            cols = slice(n * wide, (n + 1) * wide)
            resid[half * BLK : (half + 1) * BLK, cols] = seen[:, cols] + jnp.dot(
                turned, wo[:, cols], preferred_element_type=F32
            )
        whole = resid[half * BLK : (half + 1) * BLK, :]
        factor = lax.rsqrt(jnp.mean(whole * whole, axis=1, keepdims=True) + 1e-05)
        hid[half * BLK : (half + 1) * BLK, :] = (whole * factor * gain_ref[...]).astype(BF)

        def z_start(n, _):
            step = pick(n, (0,) + RING)

            @pl.when(lax.rem(lax.rem(env + step, envs), 4) // 2 == half)
            def _():
                z_copy(step).start()

            return 0

        lax.fori_loop(1, envs, z_start, 0)
    mine.start()
    own_forward(kst, kbuf, kf_send, kf_recv).wait_send()
    own_forward(vst, vbuf, vf_send, vf_recv).wait_send()
    q_send(0, 1).wait_send()

    @pl.when(core == 1)
    def _():
        sent_all()

    def finish(step, _):
        send(kst, kbuf, ks_send, ks_recv, step).wait_send()
        send(vst, vbuf, vs_send, vs_recv, step).wait_send()
        forward(kbuf, kf_send, kf_recv, step).wait_send()
        forward(vbuf, vf_send, vf_recv, step).wait_send()
        for flip in range(2):
            q_send(step, flip).wait_send()
        return 0

    lax.fori_loop(1, chips, finish, 0)

    loads[4].wait()
    loads[5].wait()
    mine.wait()
    for together in ((0, 1, 7), (2, 6), (3, 5, 4)):
        for step in together:
            if step:
                z_arrival(step).wait_recv()
        places = [lax.rem(env + envs - step, envs) for step in together]
        moved = jnp.concatenate([hbuf[at] for at in places], axis=0)
        for n in range(whead_ref.shape[1] // wide):
            cols = slice(n * wide, (n + 1) * wide)
            mixed = jnp.dot(moved, wm[:, cols], preferred_element_type=F32)
            parted = jnp.dot(moved, wg[:, cols], preferred_element_type=F32)
            for m, at in enumerate(places):
                mix[at, :, cols] = mixed[m * per_env : (m + 1) * per_env]
                part[at, :, cols] = parted[m * per_env : (m + 1) * per_env]
    partners = []
    values = []
    for e in range(envs):
        partner = jnp.int32(0)
        for f in range(envs):
            if f != e:
                partner = jnp.where(group_ref[f] == group_ref[e], f, partner)
        partners.append(partner)
        x = mix[e] + 0.5 * (part[e] + part[partner])
        activ = 0.5 * x * (1.0 + lax.erf(x * np.float32(np.sqrt(0.5))))
        values.append(jnp.sum(activ * whead_ref[...], axis=1, keepdims=True).T)
    for e in range(envs):
        val_ref[e : e + 1, :] = values[e]
    excess = ret_ref[...] - val_ref[...]
    rows = lax.broadcasted_iota(jnp.int32, (envs, per_env), 0)
    for e in range(envs):
        mine_ = excess[e : e + 1]
        other = jnp.sum(jnp.where(rows == jnp.full(rows.shape, partners[e], jnp.int32), excess, 0.0), axis=0, keepdims=True)
        adv_ref[e : e + 1, :] = mine_ - 0.5 * (mine_ + other)

    def z_finish(step, _):
        z_copy(step).wait_send()
        return 0

    lax.fori_loop(1, envs, z_finish, 0)


def decoder(rank, group_of_env, visible, obs, actions, table, gain, w_head, returns, w_query, w_key, w_value, w_out, w_mix, w_group):
    rows, width = obs.shape
    envs, per_env = returns.shape
    units = w_head.shape[0]
    blocks = rank.shape[0]
    chips = SIDE * SIDE
    groups = 2
    keys = 4 * groups * BLK
    ids = jnp.arange(blocks, dtype=jnp.int32)
    order = jnp.sum(jnp.where(rank[None, :] == ids[:, None], ids[None, :], 0), axis=1)
    sm = pl.BlockSpec(memory_space=pltpu.SMEM)
    vm = pl.BlockSpec(memory_space=pltpu.VMEM)
    hbm = pl.BlockSpec(memory_space=pl.ANY)
    dma = pltpu.SemaphoreType.DMA
    out = jax.ShapeDtypeStruct((envs, per_env), F32)
    return pl.pallas_call(
        decoder_kernel,
        out_shape=(out, out),
        in_specs=[sm] * 3 + [vm] * 7 + [hbm] * 7,
        out_specs=(vm, vm),
        scratch_shapes=[pltpu.VMEM((rows, width), BF)]
        + [pltpu.VMEM((width, width), BF)] * 4
        + [pltpu.VMEM((width, units), BF)] * 2
        + [pltpu.VMEM((rows, width), BF)]
        + [pltpu.VMEM((2, width, BLK), BF)] * 3
        + [
            pltpu.VMEM((2 * chips, HD, BLK), BF),
            pltpu.VMEM((blocks, HD, BLK), BF),
            pltpu.VMEM((blocks, HD, BLK), BF),
            pltpu.VMEM((blocks * BLK, HD + blocks), BF),
            pltpu.VMEM((blocks, VROWS, BLK), BF),
            pltpu.VMEM((blocks // 4, HD + blocks, QN), BF),
            pltpu.VMEM((groups, VROWS, QN), F32),
            pltpu.VMEM((blocks, HD, HALF), F32),
            pltpu.VMEM((2 * chips, HD, BLK), BF),
            pltpu.VMEM((groups, keys, QN), F32),
            pltpu.VMEM((groups, keys, QN), F32),
            pltpu.VMEM((EARLY, groups, keys, QN), F32),
            pltpu.VMEM((EARLY, 8, QN), F32),
            pltpu.VMEM((2, 2 * BLK, BLK), F32),
            pltpu.VMEM((2, chips, HD, BLK), BF),
            pltpu.VMEM((rows, width), F32),
            pltpu.VMEM((rows, width), BF),
            pltpu.VMEM((envs, per_env, width), BF),
            pltpu.VMEM((envs, per_env, units), F32),
            pltpu.VMEM((envs, per_env, units), F32),
            dma((6,)),
        ]
        + [dma((chips,))] * 4
        + [dma((2 * chips,))] * 2
        + [dma((chips,))] * 4
        + [dma((2 * chips,))] * 2
        + [dma((envs,))] * 2
        + [dma((6,)), pltpu.SemaphoreType.REGULAR],
        compiler_params=pltpu.CompilerParams(
            collective_id=0, has_side_effects=True, vmem_limit_bytes=60 * 2**20
        ),
        name="decoder",
    )(
        rank, order, group_of_env, rank[None, :], visible, actions, table, gain[None, :], w_head[None, :], returns,
        obs, w_query, w_key, w_value, w_out, w_mix, w_group,
    )


def on_device(
    obs_rep, actions, action_table, decode_rank, visible, w_query, w_key, w_value, w_out,
    norm_gain, w_mix, w_group, w_head, returns, group_of_env,
):
    return decoder(
        decode_rank, group_of_env, visible, obs_rep[0], actions, action_table, norm_gain, w_head, returns,
        w_query, w_key, w_value, w_out, w_mix, w_group,
    )


def solution(mesh):
    spec = P(None, ("agent", "env"))
    in_specs = (P("env", "agent", None), P("env", "agent")) + (P(),) * 11 + (spec, P())
    return jax.shard_map(
        on_device, mesh=mesh, in_specs=in_specs, out_specs=(spec, spec), check_vma=False
    )
```

```python
import jax
import jax.numpy as jnp
import numpy as np
from jax import lax
from jax.experimental import pallas as pl
from jax.experimental.pallas import tpu as pltpu
from jax.sharding import PartitionSpec as P

H = 16
BLK = 128
HALF = BLK // 2
HD = 64
LOG2E = 1.4426950408889634
NEG = -1e30
VROWS = 80
QN = 256
SIDE = 4
MESH = pl.DeviceIdType.MESH
BF = jnp.bfloat16
F32 = jnp.float32


def agent_at(y, x, core):
    return (y * SIDE + x) * 2 + core


OFFSETS = (
    (0, 1), (0, 3), (1, 0), (3, 0), (0, 2), (2, 0), (1, 1), (3, 3),
    (1, 3), (3, 1), (1, 2), (3, 2), (2, 1), (2, 3), (2, 2),
)
EARLY = 8
RING = (1, 7, 2, 6, 3, 5, 4)


def pick(n, values):
    got = jnp.int32(values[0])
    for at, value in enumerate(values[1:], 1):
        got = jnp.where(n == at, value, got)
    return got


def chip_step(n):
    return pick(n, (0,) + tuple(y * SIDE + x for y, x in OFFSETS))


def decoder_kernel(
    rank_ref, group_ref, rank_row, visible_ref, act_ref, table_ref, gain_ref, whead_ref, ret_ref,
    obs_hbm, wq_hbm, wk_hbm, wv_hbm, wo_hbm, wm_hbm, wg_hbm,
    val_ref, adv_ref,
    obs_ref, wq, wk, wv, wo, wm, wg, tok, kst, vst, qst, qbuf, kbuf, vbuf,
    order, order_vec, ks, vs, qa, acc, osort, ost, sa, sb, pre, pre_peak, mask,
    att, resid, hid, hbuf, mix, part,
    load_sem, ks_send, ks_recv, vs_send, vs_recv, qs_send, qs_recv, kf_send, kf_recv, vf_send, vf_recv,
    a_send, a_recv, z_send, z_recv, local_sem, turn_sem,
):
    groups = acc.shape[0]
    env = lax.axis_index("env")
    envs = hbuf.shape[0]
    me = lax.axis_index("agent")
    core = lax.rem(me, 2)
    chip = me // 2
    my_y, my_x = chip // SIDE, lax.rem(chip, SIDE)
    chips = SIDE * SIDE
    sibling = chip * 2 + 1 - core
    obs_load = pltpu.make_async_copy(obs_hbm, obs_ref, local_sem.at[5])
    obs_load.start()
    pairs = ((wk_hbm, wk), (wq_hbm, wq), (wv_hbm, wv), (wo_hbm, wo), (wm_hbm, wm), (wg_hbm, wg))
    loads = [pltpu.make_async_copy(src, dst, load_sem.at[n]) for n, (src, dst) in enumerate(pairs)]
    for load in loads[:3]:
        load.start()
    barrier = pltpu.get_barrier_semaphore()

    def tell(step, _):
        other = lax.rem(me + step, 2 * chips)
        pl.semaphore_signal(barrier, inc=1, device_id={"agent": other}, device_id_type=MESH)
        return 0

    def tell_env(step, _):
        other = lax.rem(env + step, envs)
        pl.semaphore_signal(barrier, inc=1, device_id={"env": other}, device_id_type=MESH)
        return 0

    lax.fori_loop(1, 2 * chips, tell, 0)
    lax.fori_loop(1, envs, tell_env, 0)

    blocks = rank_row.shape[1]
    ids_r = lax.broadcasted_iota(jnp.int32, (blocks, blocks), 0)
    ids_c = lax.broadcasted_iota(jnp.int32, (blocks, blocks), 1)
    to_rank = (ids_r == rank_row[...]).astype(F32)
    order_vec[...] = jnp.zeros_like(order_vec)
    order_vec[:, 0:blocks] = jnp.where(ids_r == rank_row[...], ids_c, 0)
    found = order_vec[...]
    for reach in (64, 32, 16, 8, 4, 2, 1):
        found = jnp.maximum(found, pltpu.roll(found, reach, 1))
    order_vec[...] = found
    order_load = pltpu.make_async_copy(order_vec, order, local_sem.at[6])
    order_load.start()

    onehot = (act_ref[...] == lax.broadcasted_iota(jnp.int32, (table_ref.shape[0], 2 * BLK), 0)).astype(F32)
    onehot = jnp.transpose(onehot).astype(BF)
    width = obs_ref.shape[1]
    strip = 256

    def embed(n, _):
        cols = pl.ds(pl.multiple_of(n * strip, strip), strip)
        added = jnp.dot(onehot, table_ref[:, cols], preferred_element_type=F32)
        tok[:, cols] = (obs_ref[:, cols].astype(F32) + added).astype(BF)
        return 0

    obs_load.wait()
    lax.fori_loop(0, width // strip, embed, 0)

    def project(rows, w, out):
        def one(n, _):
            cols = pl.ds(pl.multiple_of(n * strip, strip), strip)
            got = jnp.dot(rows, w[:, cols], preferred_element_type=F32).astype(BF)
            turned = jnp.transpose(got)
            out[0, cols, :] = turned[:, :BLK]
            out[1, cols, :] = turned[:, BLK:]
            return 0

        lax.fori_loop(0, width // strip, one, 0)

    def there(step):
        return lax.rem(my_y + step // SIDE, SIDE), lax.rem(my_x + lax.rem(step, SIDE), SIDE)

    def back(step):
        return lax.rem(my_y + SIDE - step // SIDE, SIDE), lax.rem(my_x + SIDE - lax.rem(step, SIDE), SIDE)

    def head_rows(y, x):
        return pl.ds(pl.multiple_of((y * SIDE + x) * HD, HD), HD)

    def send(stage, buf, sends, recvs, step):
        y, x = there(step)
        return pltpu.make_async_remote_copy(
            src_ref=stage.at[:, head_rows(y, x), :],
            dst_ref=buf.at[pl.ds(me * 2, 2)],
            send_sem=sends.at[step], recv_sem=recvs.at[step],
            device_id={"agent": agent_at(y, x, core)}, device_id_type=MESH,
        )

    def arrival(stage, buf, sends, recvs, step):
        y, x = back(step)
        return pltpu.make_async_remote_copy(
            src_ref=stage.at[:, head_rows(y, x), :],
            dst_ref=buf.at[pl.ds(agent_at(y, x, core) * 2, 2)],
            send_sem=sends.at[step], recv_sem=recvs.at[step],
            device_id={"agent": agent_at(y, x, core)}, device_id_type=MESH,
        )

    def own_forward(stage, buf, sends, recvs):
        return pltpu.make_async_remote_copy(
            src_ref=stage.at[:, head_rows(my_y, my_x), :],
            dst_ref=buf.at[pl.ds(me * 2, 2)],
            send_sem=sends.at[0], recv_sem=recvs.at[0],
            device_id={"agent": sibling}, device_id_type=MESH,
        )

    def forward(buf, sends, recvs, step):
        y, x = back(step)
        slot = pl.ds(agent_at(y, x, core) * 2, 2)
        return pltpu.make_async_remote_copy(
            src_ref=buf.at[slot], dst_ref=buf.at[slot],
            send_sem=sends.at[step], recv_sem=recvs.at[step],
            device_id={"agent": sibling}, device_id_type=MESH,
        )

    def forwarded(buf, sends, recvs, step):
        y, x = back(step)
        slot = pl.ds(agent_at(y, x, 1 - core) * 2, 2)
        return pltpu.make_async_remote_copy(
            src_ref=buf.at[slot], dst_ref=buf.at[slot],
            send_sem=sends.at[step], recv_sem=recvs.at[step],
            device_id={"agent": sibling}, device_id_type=MESH,
        )

    def local(stage, buf, n):
        return pltpu.make_async_copy(
            stage.at[:, head_rows(my_y, my_x), :], buf.at[pl.ds(me * 2, 2)], local_sem.at[n]
        )

    def send_all(stage, buf, sends, recvs, fsends, frecvs, n):
        local(stage, buf, n).start()
        own_forward(stage, buf, fsends, frecvs).start()

        def one(n, _):
            send(stage, buf, sends, recvs, chip_step(n)).start()
            return 0

        lax.fori_loop(1, chips, one, 0)

    def q_send(step, flip):
        y, x = there(step)
        target = lax.rem(core + flip, 2)
        return pltpu.make_async_remote_copy(
            src_ref=qst.at[target, head_rows(y, x), :],
            dst_ref=qbuf.at[me],
            send_sem=qs_send.at[flip * chips + step], recv_sem=qs_recv.at[flip * chips + step],
            device_id={"agent": agent_at(y, x, target)}, device_id_type=MESH,
        )

    def q_arrival(step, flip):
        y, x = back(step)
        source = agent_at(y, x, lax.rem(core + flip, 2))
        return pltpu.make_async_remote_copy(
            src_ref=qst.at[core, head_rows(y, x), :],
            dst_ref=qbuf.at[source],
            send_sem=qs_send.at[flip * chips + step], recv_sem=qs_recv.at[flip * chips + step],
            device_id={"agent": source}, device_id_type=MESH,
        )

    loads[0].wait()
    project(tok[...], wk, kst)
    pl.semaphore_wait(barrier, 2 * chips - 1 + envs - 1)
    for load in loads[3:]:
        load.start()
    send_all(kst, kbuf, ks_send, ks_recv, kf_send, kf_recv, 0)
    rows = jnp.concatenate(
        [obs_ref[0:HALF], obs_ref[BLK : BLK + HALF], obs_ref[HALF:BLK], obs_ref[BLK + HALF :]], axis=0
    )
    loads[1].wait()
    project(rows, wq, qst)
    q_local = pltpu.make_async_copy(qst.at[core, head_rows(my_y, my_x), :], qbuf.at[me], local_sem.at[2])
    q_local.start()
    q_send(0, 1).start()

    def q_one(n, _):
        step = chip_step(n)
        q_send(step, 0).start()
        q_send(step, 1).start()
        return 0

    lax.fori_loop(1, chips, q_one, 0)

    loads[2].wait()
    project(tok[...], wv, vst)
    send_all(vst, vbuf, vs_send, vs_recv, vf_send, vf_recv, 1)
    def pass_on(stage, buf, sends, recvs, fsends, frecvs):
        def one(n, _):
            step = chip_step(n)
            arrival(stage, buf, sends, recvs, step).wait_recv()
            forward(buf, fsends, frecvs, step).start()
            return 0

        def two(step, _):
            forwarded(buf, fsends, frecvs, step).wait_recv()
            return 0

        lax.fori_loop(1, chips, one, 0)
        lax.fori_loop(0, chips, two, 0)

    lane = lax.broadcasted_iota(jnp.int32, (BLK, HD), 1)
    row = lax.broadcasted_iota(jnp.int32, (VROWS - HD, BLK), 0)
    ones = jnp.where(row == 0, 1.0, 0.0).astype(BF)

    def prepare_keys(r, _):
        at = pl.multiple_of(r * BLK, BLK)
        hot = jnp.where(lane == r, 1.0, 0.0).astype(BF)
        ks[pl.ds(at, BLK), :] = jnp.concatenate([jnp.transpose(kbuf[order[r, 0]]), hot], axis=1)
        return 0

    def prepare_values(r, _):
        vs[r] = jnp.concatenate([vbuf[order[r, 0]], ones], axis=0)
        return 0

    to_rank = to_rank.astype(BF)
    vis = visible_ref[...].astype(F32).astype(BF)
    by_query = jnp.dot(to_rank, vis, preferred_element_type=F32).astype(BF)
    ranked = lax.dot_general(
        by_query, to_rank, (((1,), (1,)), ((), ())), preferred_element_type=F32
    )
    sees = ((ids_r > ids_c) & (ranked > 0.5)) | (ids_r == ids_c)
    sees = jnp.transpose(jnp.where(sees, 1.0, 0.0)).astype(BF)

    mrow = lax.broadcasted_iota(jnp.int32, (2 * BLK, BLK), 0)
    mcol = lax.broadcasted_iota(jnp.int32, (2 * BLK, BLK), 1)
    late = (mrow // BLK == mcol // HALF) & (lax.rem(mrow, BLK) > lax.rem(mcol, HALF) + core * HALF)
    mask[0] = jnp.zeros((2 * BLK, BLK), F32)
    mask[1] = jnp.where(late, NEG, 0.0)
    acc[...] = jnp.zeros_like(acc)

    qlane = lax.broadcasted_iota(jnp.int32, (HD, BLK), 1)
    spread_r = lax.broadcasted_iota(jnp.int32, (blocks, QN), 0)
    spread_c = lax.broadcasted_iota(jnp.int32, (blocks, QN), 1)

    def half(r, want):
        b = order[r, 0]
        x = qbuf[b // 2].astype(F32)
        return jnp.where(jnp.full(x.shape, lax.rem(b, 2), jnp.int32) == want, x, pltpu.roll(x, HALF, 1))

    def prepare_queries(t, _):
        pieces = []
        for p in range(2):
            pieces.append(jnp.where(qlane < HALF, half(4 * t + 2 * p, 0), half(4 * t + 2 * p + 1, 1)))
        turned = (jnp.concatenate(pieces, axis=1) * HD**-0.5).astype(BF)
        spread = (spread_r == 4 * t + spread_c // HALF).astype(BF)
        open_ = jnp.dot(sees, spread, preferred_element_type=F32)
        bias = jnp.where(open_ > 0.5, 0.0, NEG).astype(BF)
        qa[t] = jnp.concatenate([turned, bias], axis=0)
        return 0

    per_tile = 4 * groups
    chunk_blocks = per_tile
    keys = chunk_blocks * BLK
    tiles = blocks // per_tile

    def place_of(i):
        p, j = i // (tiles + 1), lax.rem(i, tiles + 1)
        first = j < p + 1
        return jnp.where(first, p, tiles - 1 - p), jnp.where(first, j, j - p - 1)

    order_load.wait()
    pass_on(kst, kbuf, ks_send, ks_recv, kf_send, kf_recv)
    local(kst, kbuf, 0).wait()
    lax.fori_loop(0, blocks, prepare_keys, 0, unroll=4)
    q_local.wait()
    q_arrival(0, 1).wait_recv()

    def q_land(step, _):
        q_arrival(step, 0).wait_recv()
        q_arrival(step, 1).wait_recv()
        return 0

    lax.fori_loop(1, chips, q_land, 0)
    lax.fori_loop(0, blocks // 4, prepare_queries, 0, unroll=2)

    def score(i, buf, which):
        t, c = place_of(i)
        diagonal = jnp.where(t == c, 1, 0)
        base = pl.multiple_of(c * keys, keys)
        peaks = []
        for g in which:
            full = jnp.dot(ks[pl.ds(base, keys), :], qa[t * groups + g], preferred_element_type=F32)
            peak = None
            for blk in range(0, chunk_blocks, 2):
                rows = full[blk * BLK : (blk + 2) * BLK]
                p = blk // 2 - 2 * g
                if 0 <= p < 2:
                    cols = [rows[:, :BLK], rows[:, BLK:]]
                    cols[p] = cols[p] + mask[diagonal]
                    rows = jnp.concatenate(cols, axis=1)
                buf[g, blk * BLK : (blk + 2) * BLK] = rows
                top = jnp.max(rows.reshape(2 * BLK // 8, 8, QN), axis=0)
                peak = top if peak is None else jnp.maximum(peak, top)
            peaks.append(jnp.max(peak, axis=0, keepdims=True))
        return tuple(peaks)

    def absorb(i, buf, peaks, running, which):
        t, c = place_of(i)
        new = []
        for g, peak, before in zip(which, peaks, running):
            old = jnp.where(jnp.full((1, QN), c, jnp.int32) == 0, NEG, before)
            top = jnp.maximum(old, peak)
            shrink = jnp.exp2((old - top) * LOG2E)
            expo = jnp.exp2((buf[g] - top) * LOG2E).astype(BF)
            vals = jnp.concatenate([vs[c * chunk_blocks + j] for j in range(chunk_blocks)], axis=1)
            acc[g] = acc[g] * shrink + jnp.dot(vals, expo, preferred_element_type=F32)
            new.append(top)

        return tuple(new)

    def finish_tile(i):
        t, c = place_of(i)

        @pl.when(c == t)
        def _():
            for g in range(groups):
                a = acc[g]
                out = a[:HD] / a[HD : HD + 1]
                for j in range(4):
                    osort[t * per_tile + g * 4 + j] = out[:, j * HALF : (j + 1) * HALF]

    def both(i, now, later, peaks, running):
        next_peaks, next_running = (), ()
        for g in range(groups):
            next_peaks += score(i + 1, later, (g,))
            next_running += absorb(i, now, peaks[g : g + 1], running[g : g + 1], (g,))
        finish_tile(i)
        return next_peaks, next_running

    def two(h, carry):
        peaks, running = both(2 * h, sa, sb, *carry)
        return both(2 * h + 1, sb, sa, peaks, running)

    early = pre.shape[0]

    def score_early(i, _):
        for g, peak in enumerate(score(i, pre.at[i], range(groups))):
            pre_peak[i, g : g + 1] = peak
        return 0

    lax.fori_loop(0, early, score_early, 0)
    pass_on(vst, vbuf, vs_send, vs_recv, vf_send, vf_recv)
    local(vst, vbuf, 1).wait()
    lax.fori_loop(0, blocks, prepare_values, 0, unroll=4)

    def absorb_early(i, running):
        new = ()
        for g in range(groups):
            new += absorb(i, pre.at[i], (pre_peak[i, g : g + 1],), running[g : g + 1], (g,))
        finish_tile(i)
        return new

    running = tuple(jnp.full((1, QN), NEG, F32) for _ in range(groups))
    running = lax.fori_loop(0, early, absorb_early, running)
    steps = tiles * (tiles + 1) // 2
    lax.fori_loop(early // 2, steps // 2, two, (score(early, sa, range(groups)), running))

    def o_send(step, flip):
        y = lax.rem(my_y + step // SIDE, SIDE)
        x = lax.rem(my_x + lax.rem(step, SIDE), SIDE)
        target = agent_at(y, x, lax.rem(core + flip, 2))
        return pltpu.make_async_remote_copy(
            src_ref=ost.at[target], dst_ref=att.at[core, chip],
            send_sem=a_send.at[flip * chips + step], recv_sem=a_recv.at[flip * chips + step],
            device_id={"agent": target}, device_id_type=MESH,
        )

    def o_arrival(step, flip):
        y = lax.rem(my_y + SIDE - step // SIDE, SIDE)
        x = lax.rem(my_x + SIDE - lax.rem(step, SIDE), SIDE)
        other = lax.rem(core + flip, 2)
        return pltpu.make_async_remote_copy(
            src_ref=ost.at[me], dst_ref=att.at[other, y * SIDE + x],
            send_sem=a_send.at[flip * chips + step], recv_sem=a_recv.at[flip * chips + step],
            device_id={"agent": agent_at(y, x, other)}, device_id_type=MESH,
        )

    def unsort(target):
        pair = [osort[rank_ref[2 * target]], osort[rank_ref[2 * target + 1]]]
        ost[target] = jnp.concatenate(pair, axis=1).astype(BF)

    own = pltpu.make_async_copy(ost.at[me], att.at[core, chip], local_sem.at[3])

    def start(n, _):
        step = chip_step(n)
        o_send(step, 0).start()
        o_send(step, 1).start()
        return 0

    def sent(step, _):
        o_send(step, 0).wait_send()
        o_send(step, 1).wait_send()
        return 0

    def unsort_all(a, _):
        unsort(a)
        return 0

    def start_all():
        o_send(0, 1).start()
        own.start()
        lax.fori_loop(1, chips, start, 0)

    def sent_all():
        o_send(0, 1).wait_send()
        lax.fori_loop(1, chips, sent, 0)

    def place_and_start(n, _):
        step = chip_step(n)
        y, x = there(step)
        unsort(agent_at(y, x, 0))
        unsort(agent_at(y, x, 1))
        o_send(step, 0).start()
        o_send(step, 1).start()
        return 0

    @pl.when(core == 0)
    def _():
        lax.fori_loop(1, chips, place_and_start, 0)
        unsort(sibling)
        unsort(me)
        o_send(0, 1).start()
        own.start()
        sent_all()
        pl.semaphore_signal(turn_sem, inc=1, device_id={"agent": sibling}, device_id_type=MESH)

    @pl.when(core == 1)
    def _():
        lax.fori_loop(0, 2 * chips, unsort_all, 0, unroll=2)
        pl.semaphore_wait(turn_sem, 1)
        start_all()

    def land_from(which):
        flip = jnp.where(core == which, 0, 1)

        @pl.when(core == which)
        def _():
            own.wait()

        @pl.when(core != which)
        def _():
            o_arrival(0, 1).wait_recv()

        def land(step, _):
            o_arrival(step, flip).wait_recv()
            return 0

        lax.fori_loop(1, chips, land, 0)

    wide = 256
    per_env = 2 * BLK // envs

    def piece(e):
        quarter = lax.rem(e, 4)
        return pl.ds(pl.multiple_of(quarter // 2 * BLK + e // 4 * HALF + lax.rem(quarter, 2) * per_env, per_env), per_env)

    def z_copy(step):
        other = lax.rem(env + step, envs)
        return pltpu.make_async_remote_copy(
            src_ref=hid.at[piece(other)], dst_ref=hbuf.at[env],
            send_sem=z_send.at[step], recv_sem=z_recv.at[step],
            device_id={"env": other}, device_id_type=MESH,
        )

    def z_arrival(step):
        other = lax.rem(env + envs - step, envs)
        return pltpu.make_async_remote_copy(
            src_ref=hid.at[piece(env)], dst_ref=hbuf.at[other],
            send_sem=z_send.at[step], recv_sem=z_recv.at[step],
            device_id={"env": other}, device_id_type=MESH,
        )

    mine = pltpu.make_async_copy(hid.at[piece(env)], hbuf.at[env], local_sem.at[4])
    loads[3].wait()
    for half in range(2):
        land_from(half)
        turned = jnp.transpose(att[half].reshape(width, BLK))
        seen = jnp.concatenate(
            [obs_ref[half * HALF : (half + 1) * HALF], obs_ref[BLK + half * HALF : BLK + (half + 1) * HALF]], axis=0
        ).astype(F32)
        for n in range(width // wide):
            cols = slice(n * wide, (n + 1) * wide)
            resid[half * BLK : (half + 1) * BLK, cols] = seen[:, cols] + jnp.dot(
                turned, wo[:, cols], preferred_element_type=F32
            )
        whole = resid[half * BLK : (half + 1) * BLK, :]
        factor = lax.rsqrt(jnp.mean(whole * whole, axis=1, keepdims=True) + 1e-05)
        hid[half * BLK : (half + 1) * BLK, :] = (whole * factor * gain_ref[...]).astype(BF)

        def z_start(n, _):
            step = pick(n, (0,) + RING)

            @pl.when(lax.rem(lax.rem(env + step, envs), 4) // 2 == half)
            def _():
                z_copy(step).start()

            return 0

        lax.fori_loop(1, envs, z_start, 0)
    mine.start()
    own_forward(kst, kbuf, kf_send, kf_recv).wait_send()
    own_forward(vst, vbuf, vf_send, vf_recv).wait_send()
    q_send(0, 1).wait_send()

    @pl.when(core == 1)
    def _():
        sent_all()

    def finish(step, _):
        send(kst, kbuf, ks_send, ks_recv, step).wait_send()
        send(vst, vbuf, vs_send, vs_recv, step).wait_send()
        forward(kbuf, kf_send, kf_recv, step).wait_send()
        forward(vbuf, vf_send, vf_recv, step).wait_send()
        for flip in range(2):
            q_send(step, flip).wait_send()
        return 0

    lax.fori_loop(1, chips, finish, 0)

    loads[4].wait()
    loads[5].wait()
    mine.wait()
    for together in ((0, 1, 7), (2, 6), (3, 5, 4)):
        for step in together:
            if step:
                z_arrival(step).wait_recv()
        places = [lax.rem(env + envs - step, envs) for step in together]
        moved = jnp.concatenate([hbuf[at] for at in places], axis=0)
        for n in range(whead_ref.shape[1] // wide):
            cols = slice(n * wide, (n + 1) * wide)
            mixed = jnp.dot(moved, wm[:, cols], preferred_element_type=F32)
            parted = jnp.dot(moved, wg[:, cols], preferred_element_type=F32)
            for m, at in enumerate(places):
                mix[at, :, cols] = mixed[m * per_env : (m + 1) * per_env]
                part[at, :, cols] = parted[m * per_env : (m + 1) * per_env]
    partners = []
    values = []
    for e in range(envs):
        partner = jnp.int32(0)
        for f in range(envs):
            if f != e:
                partner = jnp.where(group_ref[f] == group_ref[e], f, partner)
        partners.append(partner)
        x = mix[e] + 0.5 * (part[e] + part[partner])
        activ = 0.5 * x * (1.0 + lax.erf(x * np.float32(np.sqrt(0.5))))
        values.append(jnp.sum(activ * whead_ref[...], axis=1, keepdims=True).T)
    for e in range(envs):
        val_ref[e : e + 1, :] = values[e]
    excess = ret_ref[...] - val_ref[...]
    rows = lax.broadcasted_iota(jnp.int32, (envs, per_env), 0)
    for e in range(envs):
        mine_ = excess[e : e + 1]
        other = jnp.sum(jnp.where(rows == jnp.full(rows.shape, partners[e], jnp.int32), excess, 0.0), axis=0, keepdims=True)
        adv_ref[e : e + 1, :] = mine_ - 0.5 * (mine_ + other)

    def z_finish(step, _):
        z_copy(step).wait_send()
        return 0

    lax.fori_loop(1, envs, z_finish, 0)


def decoder(rank, group_of_env, visible, obs, actions, table, gain, w_head, returns, w_query, w_key, w_value, w_out, w_mix, w_group):
    rows, width = obs.shape
    envs, per_env = returns.shape
    units = w_head.shape[0]
    blocks = rank.shape[0]
    chips = SIDE * SIDE
    groups = 2
    keys = 4 * groups * BLK
    sm = pl.BlockSpec(memory_space=pltpu.SMEM)
    vm = pl.BlockSpec(memory_space=pltpu.VMEM)
    hbm = pl.BlockSpec(memory_space=pl.ANY)
    dma = pltpu.SemaphoreType.DMA
    out = jax.ShapeDtypeStruct((envs, per_env), F32)
    return pl.pallas_call(
        decoder_kernel,
        out_shape=(out, out),
        in_specs=[sm] * 2 + [vm] * 7 + [hbm] * 7,
        out_specs=(vm, vm),
        scratch_shapes=[pltpu.VMEM((rows, width), BF)]
        + [pltpu.VMEM((width, width), BF)] * 4
        + [pltpu.VMEM((width, units), BF)] * 2
        + [pltpu.VMEM((rows, width), BF)]
        + [pltpu.VMEM((2, width, BLK), BF)] * 3
        + [
            pltpu.VMEM((2 * chips, HD, BLK), BF),
            pltpu.VMEM((blocks, HD, BLK), BF),
            pltpu.VMEM((blocks, HD, BLK), BF),
            pltpu.SMEM((blocks, 128), jnp.int32),
            pltpu.VMEM((blocks, 128), jnp.int32),
            pltpu.VMEM((blocks * BLK, HD + blocks), BF),
            pltpu.VMEM((blocks, VROWS, BLK), BF),
            pltpu.VMEM((blocks // 4, HD + blocks, QN), BF),
            pltpu.VMEM((groups, VROWS, QN), F32),
            pltpu.VMEM((blocks, HD, HALF), F32),
            pltpu.VMEM((2 * chips, HD, BLK), BF),
            pltpu.VMEM((groups, keys, QN), F32),
            pltpu.VMEM((groups, keys, QN), F32),
            pltpu.VMEM((EARLY, groups, keys, QN), F32),
            pltpu.VMEM((EARLY, 8, QN), F32),
            pltpu.VMEM((2, 2 * BLK, BLK), F32),
            pltpu.VMEM((2, chips, HD, BLK), BF),
            pltpu.VMEM((rows, width), F32),
            pltpu.VMEM((rows, width), BF),
            pltpu.VMEM((envs, per_env, width), BF),
            pltpu.VMEM((envs, per_env, units), F32),
            pltpu.VMEM((envs, per_env, units), F32),
            dma((6,)),
        ]
        + [dma((chips,))] * 4
        + [dma((2 * chips,))] * 2
        + [dma((chips,))] * 4
        + [dma((2 * chips,))] * 2
        + [dma((envs,))] * 2
        + [dma((7,)), pltpu.SemaphoreType.REGULAR],
        compiler_params=pltpu.CompilerParams(
            collective_id=0, has_side_effects=True, vmem_limit_bytes=60 * 2**20
        ),
        name="decoder",
    )(
        rank, group_of_env, rank[None, :], visible, actions, table, gain[None, :], w_head[None, :], returns,
        obs, w_query, w_key, w_value, w_out, w_mix, w_group,
    )


def on_device(
    obs_rep, actions, action_table, decode_rank, visible, w_query, w_key, w_value, w_out,
    norm_gain, w_mix, w_group, w_head, returns, group_of_env,
):
    return decoder(
        decode_rank, group_of_env, visible, obs_rep[0], actions, action_table, norm_gain, w_head, returns,
        w_query, w_key, w_value, w_out, w_mix, w_group,
    )


def solution(mesh):
    spec = P(None, ("agent", "env"))
    in_specs = (P("env", "agent", None), P("env", "agent")) + (P(),) * 11 + (spec, P())
    return jax.shard_map(
        on_device, mesh=mesh, in_specs=in_specs, out_specs=(spec, spec), check_vma=False
    )
```
